256 devices in a mesh: ctx: 64 (over z, x, y_lo), rep: 4 (over y_hi, core).
Axes of the slice: x: 4, y: 4 (y_hi: 2, y_lo: 2; y = y_hi * 2 + y_lo), z: 8, core: 2. Of those that a mesh axis runs over, the one named last changes fastest.
Arguments:
- gated_input: bfloat16 [8, 256, 32768], P('rep', None, 'ctx'), may hold values from -6 to 6
- out_grad: bfloat16 [8, 256, 32768], P('rep', None, 'ctx'), may hold values from -6 to 6
- filter_taps: float32 [256, 32768], P('ctx'), may hold values from -1 to 1
Outputs:
- input_grad: bfloat16 [8, 256, 32768], P('rep', None, 'ctx')
- filter_grad: float32 [256, 32768], P(('ctx', 'rep'))
The draws below stay inside these ranges and needn't reach their ends.
All inputs are finite; a program needn't handle non-finite values.
Results may differ from the reference program's by a relative error of at most 0.002.
Values may be sent and summed in bfloat16 or wider, within the bound.
A program may use at most 128 MiB of HBM per device.

```python
import math
import jax
import jax.numpy as jnp
from jax import lax

LENGTH = 32768
CH = 256
BATCH = 8


def draw_filter_taps(key, part):
    key = jax.random.fold_in(key, 7)
    decay_key, noise_key = jax.random.split(key)
    low_decay = 32.0
    high_decay = 2.0 * LENGTH
    noise = jnp.clip(jax.random.normal(noise_key, (CH, LENGTH), jnp.float32), -3.0, 3.0)
    log_decay = jax.random.uniform(decay_key, (CH, 1), jnp.float32, math.log(low_decay), math.log(high_decay))
    decay = jnp.exp(log_decay)
    lag_values = jnp.arange(LENGTH, dtype=jnp.int32).astype(jnp.float32)[None, :]
    ratio = jnp.exp(-1.0 / decay)
    envelope = jnp.exp(-lag_values / decay) * jnp.sqrt(1.0 - ratio * ratio)
    return (noise * envelope).astype(jnp.float32)


def level_of(own_key, shape, cuts, least, top_value):
    loudness = 1.0
    for axis_at, parts in cuts:
        draws = jax.random.uniform(jax.random.fold_in(jax.random.fold_in(own_key, 6), axis_at), (parts,), jnp.float32, least / len(cuts), top_value / len(cuts))
        loudness = loudness * jnp.repeat(jnp.exp(draws), shape[axis_at] // parts).reshape((-1,) + (1,) * (len(shape) - 1 - axis_at))
    return loudness


def scatter_about(key, shape, width, limit, cuts=(), kind=jnp.bfloat16):
    result = jax.random.normal(key, shape, jnp.float32) * width
    if len(cuts) > 0:
        result = level_of(key, shape, cuts, -0.22, 0.18) * result
    return jnp.clip(result, min=-limit, max=limit).astype(kind)


def setup_inputs(seed: int = 0) -> dict:
    arg_keys = jax.random.split(jax.random.key(seed), 4)
    return {
        "gated_input": scatter_about(arg_keys[0], (BATCH, CH, LENGTH), 1.0, 6.0, ((0, 4), (2, 64))),
        "out_grad": scatter_about(arg_keys[1], (BATCH, CH, LENGTH), 1.0, 6.0, ((0, 4), (2, 64))),
        "filter_taps": draw_filter_taps(jax.random.fold_in(arg_keys[3], 71), 0),
    }


def group_grads(pieces):
    inputs_blk, grads_blk, filter_blk = pieces
    fft_len = 2 * LENGTH
    spec_filter = jnp.fft.rfft(filter_blk, n=fft_len, axis=-1)
    spec_input = jnp.fft.rfft(inputs_blk, n=fft_len, axis=-1)
    spec_grad = jnp.fft.rfft(grads_blk, n=fft_len, axis=-1)
    input_corr = jnp.fft.irfft(jnp.conj(spec_filter)[None] * spec_grad, n=fft_len, axis=-1)[..., :LENGTH]
    cross_sum = lax.optimization_barrier(jnp.sum(jnp.conj(spec_input) * spec_grad, axis=0))
    filter_corr = jnp.fft.irfft(cross_sum, n=fft_len, axis=-1)[..., :LENGTH]
    return (input_corr, filter_corr)

def reference(gated_input, out_grad, filter_taps):
    group_size = 16
    groups = CH // group_size
    inputs_ch = gated_input.astype(jnp.float32)
    grads_ch = out_grad.astype(jnp.float32)
    inputs_grp = jnp.swapaxes(inputs_ch.reshape(BATCH, groups, group_size, LENGTH), 0, 1)
    grads_grp = jnp.swapaxes(grads_ch.reshape(BATCH, groups, group_size, LENGTH), 0, 1)
    filter_grp = filter_taps.reshape(groups, group_size, LENGTH)
    input_corr, filter_corr = lax.map(group_grads, (inputs_grp, grads_grp, filter_grp))
    input_corr = jnp.swapaxes(input_corr, 0, 1).reshape(BATCH, CH, LENGTH)
    input_grad = input_corr.astype(jnp.bfloat16)
    filter_corr = filter_corr.reshape(CH, LENGTH)
    filter_grad = (filter_corr * (1.0 / math.sqrt(BATCH * LENGTH))).astype(jnp.float32)
    return (input_grad, filter_grad)
```

```python
import functools
import math

import jax
import jax.numpy as jnp
import ml_dtypes
import numpy as np
from jax import lax
from jax.experimental import pallas as pl
from jax.experimental.pallas import tpu as pltpu
from jax.sharding import PartitionSpec as P

MESH = pl.DeviceIdType.MESH
CTX = 64
REP = 4
ROWS = 16
F32 = jnp.float32
BF16 = jnp.bfloat16

P1, P3, P2, A2, DHI, DLO, EHI, ELO, BB = range(9)


def split16(table):
    high = table.astype(ml_dtypes.bfloat16)
    low = (table - high.astype(np.float64)).astype(ml_dtypes.bfloat16)
    return high, low


def bf16_tables():
    out = np.zeros((9, 256, 256), ml_dtypes.bfloat16)
    for chan in range(64):
        for seq in range(2):
            for half in range(2):
                row = (chan // 4) * 16 + seq * 8 + (chan % 4) * 2 + half
                col = seq * 128 + half * 64 + chan
                out[P1, row, col] = 1
                out[P3, col, row] = 1
    for at in range(256):
        out[P2, (at % 16) * 16 + at // 16, at] = 1
    place = np.arange(128)
    pos = 2 * (place % 64) + place // 64
    k1 = np.arange(128)
    angle = 2 * math.pi * ((pos[None, :] * (2 * k1[:, None] + 1)) % 512) / 512
    first = np.concatenate([np.cos(angle), -np.sin(angle)], 0)
    high, low = split16(first)
    out[A2] = np.concatenate([high, low], 1)
    high, low = split16(first.T * 2.0**-15)
    out[BB] = np.concatenate([high, low], 0)
    turn = 2 * math.pi * ((k1[:, None] * k1[None, :]) % 128) / 128
    cos, sin = np.cos(turn), np.sin(turn)
    out[DHI], out[DLO] = split16(np.block([[cos, -sin], [sin, cos]]))
    out[EHI], out[ELO] = split16(np.block([[cos, sin], [-sin, cos]]))
    return out


def f32_tables():
    k1 = np.arange(128)[:, None]
    q = np.arange(256)[None, :]
    angle = 2 * math.pi * (q * (2 * k1 + 1)) / 131072
    half = np.broadcast_to(2 * math.pi * np.arange(128)[None, :] / 256, (128, 128))
    return np.concatenate(
        [np.cos(angle), -np.sin(angle), np.cos(half), -np.sin(half)], 1
    ).astype(np.float32)


def dot(left, right):
    return jnp.dot(left, right, preferred_element_type=F32)


def halves(value):
    high = value.astype(BF16)
    return high, (value - high.astype(F32)).astype(BF16)


def cmul(ar, ai, br, bi):
    return ar * br - ai * bi, ar * bi + ai * br


def forward_tail(tab, tw, step):
    t0r, t1r = tw[:, 0:128], tw[:, 128:256]
    t0i, t1i = tw[:, 256:384], tw[:, 384:512]
    wr, wi = tw[:, 512:640], tw[:, 640:768]
    z0r, z0i = cmul(step[:128, :128], step[128:, :128], t0r, t0i)
    z1r, z1i = cmul(step[:128, 128:], step[128:, 128:], t1r, t1i)
    odd_r, odd_i = cmul(z0r - z1r, z0i - z1i, wr, wi)
    both = jnp.concatenate(
        [
            jnp.concatenate([z0r + z1r, z0i + z1i], 1),
            jnp.concatenate([odd_r, odd_i], 1),
        ],
        0,
    )
    high, low = halves(both)
    return dot(high, tab[DHI]) + dot(low, tab[DHI]) + dot(high, tab[DLO])


def inverse(tab, tw, spec):
    high, low = halves(spec)
    back = dot(high, tab[EHI]) + dot(low, tab[EHI]) + dot(high, tab[ELO])
    t0r, t1r = tw[:, 0:128], tw[:, 128:256]
    t0i, t1i = tw[:, 256:384], tw[:, 384:512]
    wr, wi = tw[:, 512:640], tw[:, 640:768]
    er, ei = back[:128, :128], back[:128, 128:]
    dr, di = cmul(back[128:, :128], back[128:, 128:], wr, -wi)
    a0r, a0i = cmul(er + dr, ei + di, t0r, -t0i)
    a1r, a1i = cmul(er - dr, ei - di, t1r, -t1i)
    stack = jnp.concatenate(
        [jnp.concatenate([a0r, a1r], 1), jnp.concatenate([a0i, a1i], 1)], 0
    )
    high, low = halves(stack)
    wide = dot(tab[BB], high)
    return wide[:128] + wide[128:] + dot(tab[BB, :128, :], low)


def kernel(
    og_hbm, gi_hbm, flt_hbm, tab_hbm, tw_hbm,
    ig_out, fg_out,
    og_in, gi_in, flt, tab, tw,
    og_send, gi_send, ig_send, og_recv, gi_recv, ig_recv,
    rows, grad_spec, flt_spec, fg_part, fg_recv,
    in_sem, send_sem, recv_sem, fg_send_sem, fg_recv_sem,
):
    me = lax.axis_index("ctx")
    rep = lax.axis_index("rep")

    loads = [
        pltpu.make_async_copy(src, dst, in_sem.at[at])
        for at, (src, dst) in enumerate(
            ((og_hbm, og_in), (tab_hbm, tab), (gi_hbm, gi_in), (flt_hbm, flt), (tw_hbm, tw))
        )
    ]
    for load in loads:
        load.start()

    barrier = pltpu.get_barrier_semaphore()

    def greet(step, _):
        pl.semaphore_signal(
            barrier, inc=1, device_id={"ctx": lax.rem(me + step, CTX)}, device_id_type=MESH
        )
        return 0

    lax.fori_loop(1, CTX, greet, 0)
    for step in range(1, REP):
        pl.semaphore_signal(
            barrier, inc=1, device_id={"rep": lax.rem(rep + step, REP)}, device_id_type=MESH
        )

    def arrange(source, target):
        def group(at, _):
            chans = pl.ds(pl.multiple_of(at * 64, 64), 64)
            block = jnp.concatenate(
                [
                    source[seq, chans, half * 256 : half * 256 + 256]
                    for seq in range(2)
                    for half in range(2)
                ],
                0,
            )
            target[pl.ds(pl.multiple_of(at * 256, 256), 256), :] = dot(tab[P1], block).astype(BF16)
            return 0

        lax.fori_loop(0, 4, group, 0)

    mine = pl.ds(pl.multiple_of(me * ROWS, ROWS), ROWS)

    def send_all(source, target, which):
        def send(step, _):
            to = lax.rem(me + step, CTX)
            pltpu.make_async_remote_copy(
                src_ref=source.at[pl.ds(pl.multiple_of(to * ROWS, ROWS), ROWS), :],
                dst_ref=target.at[mine, :],
                send_sem=send_sem.at[which],
                recv_sem=recv_sem.at[which],
                device_id={"ctx": to},
                device_id_type=MESH,
            ).start()
            return 0

        lax.fori_loop(1, CTX, send, 0)
        target[mine, :] = source[mine, :]

    def wait_all(buffer, sems, which):
        part = buffer.at[pl.ds(0, (CTX - 1) * ROWS), :]
        pltpu.make_async_copy(part, part, sems.at[which]).wait()

    loads[0].wait()
    loads[1].wait()
    arrange(og_in, og_send)
    pl.semaphore_wait(barrier, CTX - 1 + REP - 1)
    send_all(og_send, og_recv, 0)
    loads[2].wait()
    arrange(gi_in, gi_send)
    send_all(gi_send, gi_recv, 1)
    loads[3].wait()
    loads[4].wait()

    def filter_spectrum(chan, _):
        taps = jnp.concatenate(
            [
                jnp.concatenate(
                    [flt[pl.ds(8 * half + 4 * high + chan, 64, stride=16), :] for high in range(2)], 1
                )
                for half in range(2)
            ],
            0,
        )
        high, low = halves(taps)
        step = dot(tab[A2], jnp.concatenate([high, high], 0)) + dot(tab[A2, :, :128], low)
        flt_spec[chan] = forward_tail(tab, tw, step)
        return 0

    lax.fori_loop(0, 4, filter_spectrum, 0)

    def to_rows(buffer):
        def group(at, _):
            block = buffer[pl.ds(pl.multiple_of(at * 256, 256), 256), :]
            turned = dot(tab[P2], block).astype(BF16)
            for row in range(16):
                rows[pl.ds(pl.multiple_of(row * 64 + at * 16, 16), 16), :] = turned[row * 16 : row * 16 + 16]
            return 0

        lax.fori_loop(0, 4, group, 0)

    def spectrum(at):
        block = rows[pl.ds(pl.multiple_of(at * 128, 128), 128), :]
        return forward_tail(tab, tw, dot(tab[A2], jnp.concatenate([block, block], 0)))

    wait_all(og_recv, recv_sem, 0)
    to_rows(og_recv)

    def input_grad(at, _):
        spec = spectrum(at)
        grad_spec[at] = spec
        taps = flt_spec[lax.rem(at, 4)]
        sr, si, fr, fi = spec[:, :128], spec[:, 128:], taps[:, :128], taps[:, 128:]
        corr = jnp.concatenate([fr * sr + fi * si, fr * si - fi * sr], 1)
        rows[pl.ds(pl.multiple_of(at * 128, 128), 128), :] = inverse(tab, tw, corr).astype(BF16)
        return 0

    lax.fori_loop(0, 8, input_grad, 0)

    def from_rows(at, _):
        block = jnp.concatenate(
            [rows[pl.ds(pl.multiple_of(row * 64 + at * 16, 16), 16), :] for row in range(16)], 0
        )
        ig_send[pl.ds(pl.multiple_of(at * 256, 256), 256), :] = dot(tab[P2], block).astype(BF16)
        return 0

    lax.fori_loop(0, 4, from_rows, 0)
    send_all(ig_send, ig_recv, 2)

    wait_all(gi_recv, recv_sem, 1)
    to_rows(gi_recv)

    def filter_grad(chan, _):
        total_r = total_i = None
        for seq in range(2):
            at = chan + 4 * seq
            spec = spectrum(at)
            grad = grad_spec[at]
            sr, si, gr, gi = spec[:, :128], spec[:, 128:], grad[:, :128], grad[:, 128:]
            real, imag = sr * gr + si * gi, sr * gi - si * gr
            total_r = real if total_r is None else total_r + real
            total_i = imag if total_i is None else total_i + imag
        fg_part[chan] = inverse(tab, tw, jnp.concatenate([total_r, total_i], 1))
        return 0

    lax.fori_loop(0, 4, filter_grad, 0)

    for step in range(1, REP):
        to = lax.rem(rep + step, REP)
        pltpu.make_async_remote_copy(
            src_ref=fg_part.at[to],
            dst_ref=fg_recv.at[step - 1],
            send_sem=fg_send_sem.at[step - 1],
            recv_sem=fg_recv_sem.at[step - 1],
            device_id={"rep": to},
            device_id_type=MESH,
        ).start()
    total = fg_part[rep]
    for step in range(1, REP):
        slot = fg_recv.at[step - 1]
        pltpu.make_async_copy(slot, slot, fg_recv_sem.at[step - 1]).wait()
        total = total + fg_recv[step - 1]
    total = total * (1.0 / 512.0)
    for half in range(2):
        for high in range(2):
            fg_out[pl.ds(2 * half + high, 64, stride=4), :] = total[
                half * 64 : half * 64 + 64, high * 128 : high * 128 + 128
            ]

    wait_all(ig_recv, recv_sem, 2)

    def finish(at, _):
        block = ig_recv[pl.ds(pl.multiple_of(at * 256, 256), 256), :]
        turned = dot(tab[P3], block).astype(BF16)
        chans = pl.ds(pl.multiple_of(at * 64, 64), 64)
        for seq in range(2):
            for half in range(2):
                start = seq * 128 + half * 64
                ig_out[seq, chans, half * 256 : half * 256 + 256] = turned[start : start + 64]
        return 0

    lax.fori_loop(0, 4, finish, 0)
    wait_all(og_send, send_sem, 0)
    wait_all(gi_send, send_sem, 1)
    wait_all(ig_send, send_sem, 2)
    for step in range(1, REP):
        slot = fg_part.at[step - 1]
        pltpu.make_async_copy(slot, slot, fg_send_sem.at[step - 1]).wait()


def local(gated_input, out_grad, filter_taps):
    taps = filter_taps.reshape(4, 256, 128).transpose(1, 0, 2).reshape(1024, 128)
    any_spec = pl.BlockSpec(memory_space=pl.ANY)
    vmem = pl.BlockSpec(memory_space=pltpu.VMEM)
    chunks = pltpu.VMEM((CTX * ROWS, 256), BF16)
    input_grad, filter_grad = pl.pallas_call(
        kernel,
        out_shape=(
            jax.ShapeDtypeStruct((2, 256, 512), BF16),
            jax.ShapeDtypeStruct((256, 128), F32),
        ),
        in_specs=[any_spec] * 5,
        out_specs=(vmem, vmem),
        scratch_shapes=[
            pltpu.VMEM((2, 256, 512), BF16),
            pltpu.VMEM((2, 256, 512), BF16),
            pltpu.VMEM((1024, 128), F32),
            pltpu.VMEM((9, 256, 256), BF16),
            pltpu.VMEM((128, 768), F32),
            chunks, chunks, chunks, chunks, chunks, chunks,
            chunks,
            pltpu.VMEM((8, 256, 256), F32),
            pltpu.VMEM((4, 256, 256), F32),
            pltpu.VMEM((4, 128, 256), F32),
            pltpu.VMEM((3, 128, 256), F32),
            pltpu.SemaphoreType.DMA((5,)),
            pltpu.SemaphoreType.DMA((3,)),
            pltpu.SemaphoreType.DMA((3,)),
            pltpu.SemaphoreType.DMA((3,)),
            pltpu.SemaphoreType.DMA((3,)),
        ],
        compiler_params=pltpu.CompilerParams(
            collective_id=0, has_side_effects=True, vmem_limit_bytes=48 * 2**20
        ),
    )(out_grad, gated_input, taps, jnp.asarray(bf16_tables()), jnp.asarray(f32_tables()))
    return input_grad, filter_grad.reshape(1, 32768)


def solution(mesh):
    return jax.shard_map(
        local,
        mesh=mesh,
        in_specs=(P("rep", None, "ctx"), P("rep", None, "ctx"), P("ctx", None)),
        out_specs=(P("rep", None, "ctx"), P(("ctx", "rep"), None)),
        check_vma=False,
    )
```

```python
import functools
import math

import jax
import jax.numpy as jnp
import ml_dtypes
import numpy as np
from jax import lax
from jax.experimental import pallas as pl
from jax.experimental.pallas import tpu as pltpu
from jax.sharding import PartitionSpec as P

MESH = pl.DeviceIdType.MESH
CTX = 64
REP = 4
ROWS = 16
F32 = jnp.float32
BF16 = jnp.bfloat16

P1, P3, P2, A2, DHI, DLO, EHI, ELO, BB = range(-1, 8)


def split16(table):
    high = table.astype(ml_dtypes.bfloat16)
    low = (table - high.astype(np.float64)).astype(ml_dtypes.bfloat16)
    return high, low


def bf16_tables():
    out = np.zeros((9, 256, 256), ml_dtypes.bfloat16)
    move = out[P1]
    for chan in range(64):
        for seq in range(2):
            for half in range(2):
                row = (chan // 4) * 16 + seq * 8 + (chan % 4) * 2 + half
                col = seq * 128 + half * 64 + chan
                move[row, col] = 1
                out[P3, col, row] = 1
    for at in range(256):
        out[P2, (at % 16) * 16 + at // 16, at] = 1
    place = np.arange(128)
    pos = 2 * (place % 64) + place // 64
    k1 = np.arange(128)
    angle = 2 * math.pi * ((pos[None, :] * (2 * k1[:, None] + 1)) % 512) / 512
    first = np.concatenate([np.cos(angle), -np.sin(angle)], 0)
    high, low = split16(first)
    out[A2] = np.concatenate([high, low], 1)
    high, low = split16(first.T * 2.0**-15)
    out[BB] = np.concatenate([high, low], 0)
    turn = 2 * math.pi * ((k1[:, None] * k1[None, :]) % 128) / 128
    cos, sin = np.cos(turn), np.sin(turn)
    out[DHI], out[DLO] = split16(np.block([[cos, -sin], [sin, cos]]))
    out[EHI], out[ELO] = split16(np.block([[cos, sin], [-sin, cos]]))
    return move, out[:8]


def f32_tables():
    k1 = np.arange(128)[:, None]
    q = np.arange(256)[None, :]
    angle = 2 * math.pi * (q * (2 * k1 + 1)) / 131072
    half = np.broadcast_to(2 * math.pi * np.arange(128)[None, :] / 256, (128, 128))
    return np.concatenate(
        [np.cos(angle), -np.sin(angle), np.cos(half), -np.sin(half)], 1
    ).astype(np.float32)


def dot(left, right):
    return jnp.dot(left, right, preferred_element_type=F32)


def halves(value):
    high = value.astype(BF16)
    return high, (value - high.astype(F32)).astype(BF16)


def cmul(ar, ai, br, bi):
    return ar * br - ai * bi, ar * bi + ai * br


def forward_tail(tab, tw, step):
    t0r, t1r = tw[:, 0:128], tw[:, 128:256]
    t0i, t1i = tw[:, 256:384], tw[:, 384:512]
    wr, wi = tw[:, 512:640], tw[:, 640:768]
    z0r, z0i = cmul(step[:128, :128], step[128:, :128], t0r, t0i)
    z1r, z1i = cmul(step[:128, 128:], step[128:, 128:], t1r, t1i)
    odd_r, odd_i = cmul(z0r - z1r, z0i - z1i, wr, wi)
    both = jnp.concatenate(
        [
            jnp.concatenate([z0r + z1r, z0i + z1i], 1),
            jnp.concatenate([odd_r, odd_i], 1),
        ],
        0,
    )
    high, low = halves(both)
    return dot(high, tab[DHI]) + dot(low, tab[DHI]) + dot(high, tab[DLO])


def inverse(tab, tw, spec):
    high, low = halves(spec)
    back = dot(high, tab[EHI]) + dot(low, tab[EHI]) + dot(high, tab[ELO])
    t0r, t1r = tw[:, 0:128], tw[:, 128:256]
    t0i, t1i = tw[:, 256:384], tw[:, 384:512]
    wr, wi = tw[:, 512:640], tw[:, 640:768]
    er, ei = back[:128, :128], back[:128, 128:]
    dr, di = cmul(back[128:, :128], back[128:, 128:], wr, -wi)
    a0r, a0i = cmul(er + dr, ei + di, t0r, -t0i)
    a1r, a1i = cmul(er - dr, ei - di, t1r, -t1i)
    stack = jnp.concatenate(
        [jnp.concatenate([a0r, a1r], 1), jnp.concatenate([a0i, a1i], 1)], 0
    )
    high, low = halves(stack)
    wide = dot(tab[BB], high)
    return wide[:128] + wide[128:] + dot(tab[BB, :128, :], low)


def kernel(
    og_hbm, gi_hbm, flt_hbm, move_hbm, tab_hbm, tw_hbm,
    ig_out, fg_out,
    og_in, gi_in, flt, move, tab, tw,
    og_send, gi_send, ig_send, og_recv, gi_recv, ig_recv,
    rows, grad_spec, flt_spec, fg_part, fg_recv,
    in_sem, send_sem, recv_sem, fg_send_sem, fg_recv_sem,
):
    me = lax.axis_index("ctx")
    rep = lax.axis_index("rep")

    loads = [
        pltpu.make_async_copy(src, dst, in_sem.at[at])
        for at, (src, dst) in enumerate(
            ((move_hbm, move), (og_hbm, og_in), (gi_hbm, gi_in), (flt_hbm, flt), (tab_hbm, tab), (tw_hbm, tw))
        )
    ]
    for load in loads:
        load.start()

    barrier = pltpu.get_barrier_semaphore()

    def greet(step, _):
        pl.semaphore_signal(
            barrier, inc=1, device_id={"ctx": lax.rem(me + step, CTX)}, device_id_type=MESH
        )
        return 0

    lax.fori_loop(1, CTX, greet, 0)
    for step in range(1, REP):
        pl.semaphore_signal(
            barrier, inc=1, device_id={"rep": lax.rem(rep + step, REP)}, device_id_type=MESH
        )

    def arrange(source, target):
        def group(at, _):
            chans = pl.ds(pl.multiple_of(at * 64, 64), 64)
            block = jnp.concatenate(
                [
                    source[seq, chans, half * 256 : half * 256 + 256]
                    for seq in range(2)
                    for half in range(2)
                ],
                0,
            )
            target[pl.ds(pl.multiple_of(at * 256, 256), 256), :] = dot(move[...], block).astype(BF16)
            return 0

        lax.fori_loop(0, 4, group, 0)

    mine = pl.ds(pl.multiple_of(me * ROWS, ROWS), ROWS)

    def send_all(source, target, which):
        def send(step, _):
            to = lax.rem(me + step, CTX)
            pltpu.make_async_remote_copy(
                src_ref=source.at[pl.ds(pl.multiple_of(to * ROWS, ROWS), ROWS), :],
                dst_ref=target.at[mine, :],
                send_sem=send_sem.at[which],
                recv_sem=recv_sem.at[which],
                device_id={"ctx": to},
                device_id_type=MESH,
            ).start()
            return 0

        lax.fori_loop(1, CTX, send, 0)
        target[mine, :] = source[mine, :]

    def wait_all(buffer, sems, which):
        part = buffer.at[pl.ds(0, (CTX - 1) * ROWS), :]
        pltpu.make_async_copy(part, part, sems.at[which]).wait()

    loads[0].wait()
    loads[1].wait()
    arrange(og_in, og_send)
    pl.semaphore_wait(barrier, CTX - 1 + REP - 1)
    send_all(og_send, og_recv, 0)
    loads[2].wait()
    arrange(gi_in, gi_send)
    send_all(gi_send, gi_recv, 1)
    loads[3].wait()
    loads[4].wait()
    loads[5].wait()

    def filter_spectrum(chan, _):
        taps = jnp.concatenate(
            [
                jnp.concatenate(
                    [flt[pl.ds(8 * half + 4 * high + chan, 64, stride=16), :] for high in range(2)], 1
                )
                for half in range(2)
            ],
            0,
        )
        high, low = halves(taps)
        step = dot(tab[A2], jnp.concatenate([high, high], 0)) + dot(tab[A2, :, :128], low)
        flt_spec[chan] = forward_tail(tab, tw, step)
        return 0

    lax.fori_loop(0, 4, filter_spectrum, 0)

    def to_rows(buffer):
        def group(at, _):
            block = buffer[pl.ds(pl.multiple_of(at * 256, 256), 256), :]
            turned = dot(tab[P2], block).astype(BF16)
            for row in range(16):
                rows[pl.ds(pl.multiple_of(row * 64 + at * 16, 16), 16), :] = turned[row * 16 : row * 16 + 16]
            return 0

        lax.fori_loop(0, 4, group, 0)

    def spectrum(at):
        block = rows[pl.ds(pl.multiple_of(at * 128, 128), 128), :]
        return forward_tail(tab, tw, dot(tab[A2], jnp.concatenate([block, block], 0)))

    wait_all(og_recv, recv_sem, 0)
    to_rows(og_recv)

    def input_grad(at, _):
        spec = spectrum(at)
        grad_spec[at] = spec
        taps = flt_spec[lax.rem(at, 4)]
        sr, si, fr, fi = spec[:, :128], spec[:, 128:], taps[:, :128], taps[:, 128:]
        corr = jnp.concatenate([fr * sr + fi * si, fr * si - fi * sr], 1)
        rows[pl.ds(pl.multiple_of(at * 128, 128), 128), :] = inverse(tab, tw, corr).astype(BF16)
        return 0

    lax.fori_loop(0, 8, input_grad, 0)

    def from_rows(at, _):
        block = jnp.concatenate(
            [rows[pl.ds(pl.multiple_of(row * 64 + at * 16, 16), 16), :] for row in range(16)], 0
        )
        ig_send[pl.ds(pl.multiple_of(at * 256, 256), 256), :] = dot(tab[P2], block).astype(BF16)
        return 0

    lax.fori_loop(0, 4, from_rows, 0)
    send_all(ig_send, ig_recv, 2)

    wait_all(gi_recv, recv_sem, 1)
    to_rows(gi_recv)

    def part_copy(step):
        return pltpu.make_async_remote_copy(
            src_ref=fg_part.at[step],
            dst_ref=fg_recv.at[step],
            send_sem=fg_send_sem.at[step],
            recv_sem=fg_recv_sem.at[step],
            device_id={"rep": lax.rem(rep + 1 + step, REP)},
            device_id_type=MESH,
        )

    def filter_grad(step, _):
        chan = lax.rem(rep + 1 + step, REP)
        total_r = total_i = None
        for seq in range(2):
            at = chan + 4 * seq
            spec = spectrum(at)
            grad = grad_spec[at]
            sr, si, gr, gi = spec[:, :128], spec[:, 128:], grad[:, :128], grad[:, 128:]
            real, imag = sr * gr + si * gi, sr * gi - si * gr
            total_r = real if total_r is None else total_r + real
            total_i = imag if total_i is None else total_i + imag
        fg_part[step] = inverse(tab, tw, jnp.concatenate([total_r, total_i], 1))

        @pl.when(step < REP - 1)
        def _():
            part_copy(step).start()

        return 0

    lax.fori_loop(0, REP, filter_grad, 0)

    total = fg_part[REP - 1]
    for step in range(REP - 1):
        part_copy(step).wait()
        total = total + fg_recv[step]
    total = total * (1.0 / 512.0)
    for half in range(2):
        for high in range(2):
            fg_out[pl.ds(2 * half + high, 64, stride=4), :] = total[
                half * 64 : half * 64 + 64, high * 128 : high * 128 + 128
            ]

    wait_all(ig_recv, recv_sem, 2)

    def finish(at, _):
        block = ig_recv[pl.ds(pl.multiple_of(at * 256, 256), 256), :]
        turned = dot(tab[P3], block).astype(BF16)
        chans = pl.ds(pl.multiple_of(at * 64, 64), 64)
        for seq in range(2):
            for half in range(2):
                start = seq * 128 + half * 64
                ig_out[seq, chans, half * 256 : half * 256 + 256] = turned[start : start + 64]
        return 0

    lax.fori_loop(0, 4, finish, 0)
    wait_all(og_send, send_sem, 0)
    wait_all(gi_send, send_sem, 1)
    wait_all(ig_send, send_sem, 2)


def local(gated_input, out_grad, filter_taps):
    move, tables = bf16_tables()
    taps = filter_taps.reshape(4, 256, 128).transpose(1, 0, 2).reshape(1024, 128)
    hbm = pl.BlockSpec(memory_space=pltpu.HBM)
    vmem = pl.BlockSpec(memory_space=pltpu.VMEM)
    chunks = pltpu.VMEM((CTX * ROWS, 256), BF16)
    input_grad, filter_grad = pl.pallas_call(
        kernel,
        out_shape=(
            jax.ShapeDtypeStruct((2, 256, 512), BF16),
            jax.ShapeDtypeStruct((256, 128), F32),
        ),
        in_specs=[hbm] * 6,
        out_specs=(vmem, vmem),
        scratch_shapes=[
            pltpu.VMEM((2, 256, 512), BF16),
            pltpu.VMEM((2, 256, 512), BF16),
            pltpu.VMEM((1024, 128), F32),
            pltpu.VMEM((256, 256), BF16),
            pltpu.VMEM((8, 256, 256), BF16),
            pltpu.VMEM((128, 768), F32),
            chunks, chunks, chunks, chunks, chunks, chunks,
            chunks,
            pltpu.VMEM((8, 256, 256), F32),
            pltpu.VMEM((4, 256, 256), F32),
            pltpu.VMEM((4, 128, 256), F32),
            pltpu.VMEM((3, 128, 256), F32),
            pltpu.SemaphoreType.DMA((6,)),
            pltpu.SemaphoreType.DMA((3,)),
            pltpu.SemaphoreType.DMA((3,)),
            pltpu.SemaphoreType.DMA((3,)),
            pltpu.SemaphoreType.DMA((3,)),
        ],
        compiler_params=pltpu.CompilerParams(
            collective_id=0, has_side_effects=True, vmem_limit_bytes=40 * 2**20
        ),
    )(
        *(
            pltpu.with_memory_space_constraint(operand, pltpu.HBM)
            for operand in (
                out_grad, gated_input, taps,
                jnp.asarray(move), jnp.asarray(tables), jnp.asarray(f32_tables()),
            )
        )
    )
    return input_grad, filter_grad.reshape(1, 32768)


def solution(mesh):
    return jax.shard_map(
        local,
        mesh=mesh,
        in_specs=(P("rep", None, "ctx"), P("rep", None, "ctx"), P("ctx", None)),
        out_specs=(P("rep", None, "ctx"), P(("ctx", "rep"), None)),
        check_vma=False,
    )
```

```python
import functools
import math

import jax
import jax.numpy as jnp
import ml_dtypes
import numpy as np
from jax import lax
from jax.experimental import pallas as pl
from jax.experimental.pallas import tpu as pltpu
from jax.sharding import PartitionSpec as P

MESH = pl.DeviceIdType.MESH
CTX = 64
REP = 4
ROWS = 16
F32 = jnp.float32
BF16 = jnp.bfloat16

P1, P3, P2, A2, DHI, DLO, EHI, ELO, BB = range(-1, 8)


def split16(table):
    high = table.astype(ml_dtypes.bfloat16)
    low = (table - high.astype(np.float64)).astype(ml_dtypes.bfloat16)
    return high, low


def bf16_tables():
    out = np.zeros((9, 256, 256), ml_dtypes.bfloat16)
    move = out[P1]
    for chan in range(64):
        for seq in range(2):
            for half in range(2):
                row = (chan // 4) * 16 + seq * 8 + (chan % 4) * 2 + half
                col = seq * 128 + half * 64 + chan
                move[row, col] = 1
                out[P3, col, row] = 1
    for at in range(256):
        out[P2, (at % 16) * 16 + at // 16, at] = 1
    place = np.arange(128)
    pos = 2 * (place % 64) + place // 64
    k1 = np.arange(128)
    angle = 2 * math.pi * ((pos[None, :] * (2 * k1[:, None] + 1)) % 512) / 512
    first = np.concatenate([np.cos(angle), -np.sin(angle)], 0)
    high, low = split16(first)
    out[A2] = np.concatenate([high, low], 1)
    high, low = split16(first.T * 2.0**-15)
    out[BB] = np.concatenate([high, low], 0)
    turn = 2 * math.pi * ((k1[:, None] * k1[None, :]) % 128) / 128
    cos, sin = np.cos(turn), np.sin(turn)
    out[DHI], out[DLO] = split16(np.block([[cos, -sin], [sin, cos]]))
    out[EHI], out[ELO] = split16(np.block([[cos, sin], [-sin, cos]]))
    return move, out[:8]


def f32_tables():
    k1 = np.arange(128)[:, None]
    q = np.arange(256)[None, :]
    angle = 2 * math.pi * (q * (2 * k1 + 1)) / 131072
    half = np.broadcast_to(2 * math.pi * np.arange(128)[None, :] / 256, (128, 128))
    return np.concatenate(
        [np.cos(angle), -np.sin(angle), np.cos(half), -np.sin(half)], 1
    ).astype(np.float32)


def dot(left, right):
    return jnp.dot(left, right, preferred_element_type=F32)


def halves(value):
    high = value.astype(BF16)
    return high, (value - high.astype(F32)).astype(BF16)


def cmul(ar, ai, br, bi):
    return ar * br - ai * bi, ar * bi + ai * br


def twiddles(tw):
    return (
        (tw[:, 0:128], tw[:, 256:384]),
        (tw[:, 128:256], tw[:, 384:512]),
        (tw[:, 512:640], tw[:, 640:768]),
    )


def transform(rows, table_high, table_low):
    count = rows.shape[0]
    high, low = halves(rows)
    wide = dot(jnp.concatenate([high, low], 0), table_high)
    return wide[:count] + wide[count:] + dot(high, table_low)


def forward(tab, tw, step, count):
    (t0r, t0i), (t1r, t1i), (wr, wi) = twiddles(tw)
    rows = []
    for at in range(count):
        lanes = 256 * at
        z0r, z0i = cmul(step[:128, lanes : lanes + 128], step[128:, lanes : lanes + 128], t0r, t0i)
        z1r, z1i = cmul(step[:128, lanes + 128 : lanes + 256], step[128:, lanes + 128 : lanes + 256], t1r, t1i)
        odd_r, odd_i = cmul(z0r - z1r, z0i - z1i, wr, wi)
        rows.append(jnp.concatenate([z0r + z1r, z0i + z1i], 1))
        rows.append(jnp.concatenate([odd_r, odd_i], 1))
    spec = transform(jnp.concatenate(rows, 0), tab[DHI], tab[DLO])
    return [spec[256 * at : 256 * at + 256] for at in range(count)]


def inverse(tab, tw, specs):
    (t0r, t0i), (t1r, t1i), (wr, wi) = twiddles(tw)
    back = transform(jnp.concatenate(specs, 0), tab[EHI], tab[ELO])
    columns = []
    for at in range(len(specs)):
        even = back[256 * at : 256 * at + 128]
        odd = back[256 * at + 128 : 256 * at + 256]
        er, ei = even[:, :128], even[:, 128:]
        dr, di = cmul(odd[:, :128], odd[:, 128:], wr, -wi)
        a0r, a0i = cmul(er + dr, ei + di, t0r, -t0i)
        a1r, a1i = cmul(er - dr, ei - di, t1r, -t1i)
        columns.append(
            jnp.concatenate(
                [jnp.concatenate([a0r, a1r], 1), jnp.concatenate([a0i, a1i], 1)], 0
            )
        )
    high, low = halves(jnp.concatenate(columns, 1))
    wide = dot(tab[BB], high)
    out = wide[:128] + wide[128:] + dot(tab[BB, :128, :], low)
    return [out[:, 256 * at : 256 * at + 256] for at in range(len(specs))]


def kernel(
    og_hbm, gi_hbm, flt_hbm, move_hbm, tab_hbm, tw_hbm,
    ig_out, fg_out,
    og_in, gi_in, flt, move, tab, tw,
    og_send, gi_send, ig_send, og_recv, gi_recv, ig_recv,
    rows, grad_spec, flt_spec, fg_part, fg_recv,
    in_sem, send_sem, recv_sem, fg_send_sem, fg_recv_sem,
):
    me = lax.axis_index("ctx")
    rep = lax.axis_index("rep")

    loads = [
        pltpu.make_async_copy(src, dst, in_sem.at[at])
        for at, (src, dst) in enumerate(
            ((move_hbm, move), (og_hbm, og_in), (gi_hbm, gi_in), (flt_hbm, flt), (tab_hbm, tab), (tw_hbm, tw))
        )
    ]
    for load in loads:
        load.start()

    barrier = pltpu.get_barrier_semaphore()

    def greet(step, _):
        pl.semaphore_signal(
            barrier, inc=1, device_id={"ctx": lax.rem(me + step, CTX)}, device_id_type=MESH
        )
        return 0

    lax.fori_loop(1, CTX, greet, 0)
    core, high_y = lax.rem(rep, 2), rep // 2
    near = 2 * high_y + 1 - core
    far = 2 * (1 - high_y) + core
    for peer in (near, far):
        pl.semaphore_signal(barrier, inc=1, device_id={"rep": peer}, device_id_type=MESH)

    def arrange(source, target):
        def group(at, _):
            chans = pl.ds(pl.multiple_of(at * 64, 64), 64)
            block = jnp.concatenate(
                [
                    source[seq, chans, half * 256 : half * 256 + 256]
                    for seq in range(2)
                    for half in range(2)
                ],
                0,
            )
            target[pl.ds(pl.multiple_of(at * 256, 256), 256), :] = dot(move[...], block).astype(BF16)
            return 0

        lax.fori_loop(0, 4, group, 0, unroll=True)

    mine = pl.ds(pl.multiple_of(me * ROWS, ROWS), ROWS)

    def send_all(source, target, which):
        def send(step, _):
            away = jnp.where(step % 2 == 1, (step + 1) // 2, CTX - step // 2)
            to = lax.rem(me + away, CTX)
            pltpu.make_async_remote_copy(
                src_ref=source.at[pl.ds(pl.multiple_of(to * ROWS, ROWS), ROWS), :],
                dst_ref=target.at[mine, :],
                send_sem=send_sem.at[which],
                recv_sem=recv_sem.at[which],
                device_id={"ctx": to},
                device_id_type=MESH,
            ).start()
            return 0

        lax.fori_loop(1, CTX, send, 0)

    def keep_own(source, target):
        target[mine, :] = source[mine, :]

    def wait_all(buffer, sems, which):
        part = buffer.at[pl.ds(0, (CTX - 1) * ROWS), :]
        pltpu.make_async_copy(part, part, sems.at[which]).wait()

    loads[0].wait()
    loads[1].wait()
    arrange(og_in, og_send)
    pl.semaphore_wait(barrier, CTX - 1 + 2)
    send_all(og_send, og_recv, 0)
    keep_own(og_send, og_recv)
    loads[2].wait()
    arrange(gi_in, gi_send)
    send_all(gi_send, gi_recv, 1)
    keep_own(gi_send, gi_recv)
    loads[3].wait()
    loads[4].wait()
    loads[5].wait()

    def filter_spectrum(chan, _):
        taps = jnp.concatenate(
            [
                jnp.concatenate(
                    [flt[pl.ds(8 * half + 4 * high + chan, 64, stride=16), :] for high in range(2)], 1
                )
                for half in range(2)
            ],
            0,
        )
        high, low = halves(taps)
        step = dot(tab[A2], jnp.concatenate([high, high], 0)) + dot(tab[A2, :, :128], low)
        (flt_spec[chan],) = forward(tab, tw, step, 1)
        return 0

    lax.fori_loop(0, 4, filter_spectrum, 0)

    def to_rows(buffer):
        def group(at, _):
            block = buffer[pl.ds(pl.multiple_of(at * 256, 256), 256), :]
            turned = dot(tab[P2], block).astype(BF16)
            for row in range(16):
                rows[pl.ds(pl.multiple_of(row * 64 + at * 16, 16), 16), :] = turned[row * 16 : row * 16 + 16]
            return 0

        lax.fori_loop(0, 4, group, 0, unroll=True)

    def spectra(ats):
        blocks = jnp.concatenate(
            [rows[pl.ds(pl.multiple_of(at * 128, 128), 128), :] for at in ats], 1
        )
        step = dot(tab[A2], jnp.concatenate([blocks, blocks], 0))
        return forward(tab, tw, step, len(ats))

    wait_all(og_recv, recv_sem, 0)
    to_rows(og_recv)

    def input_grad(chan, _):
        ats = (chan, chan + 4)
        taps = flt_spec[chan]
        fr, fi = taps[:, :128], taps[:, 128:]
        specs = spectra(ats)
        corrs = []
        for spec in specs:
            sr, si = spec[:, :128], spec[:, 128:]
            corrs.append(jnp.concatenate([fr * sr + fi * si, fr * si - fi * sr], 1))
        grads = inverse(tab, tw, corrs)
        for at, spec, grad in zip(ats, specs, grads, strict=True):
            grad_spec[at] = spec
            rows[pl.ds(pl.multiple_of(at * 128, 128), 128), :] = grad.astype(BF16)
        return 0

    lax.fori_loop(0, 4, input_grad, 0)

    def from_rows(at, _):
        block = jnp.concatenate(
            [rows[pl.ds(pl.multiple_of(row * 64 + at * 16, 16), 16), :] for row in range(16)], 0
        )
        ig_send[pl.ds(pl.multiple_of(at * 256, 256), 256), :] = dot(tab[P2], block).astype(BF16)
        return 0

    lax.fori_loop(0, 4, from_rows, 0, unroll=True)
    send_all(ig_send, ig_recv, 2)
    keep_own(ig_send, ig_recv)

    wait_all(gi_recv, recv_sem, 1)
    to_rows(gi_recv)

    def part_copy(slot, peer):
        return pltpu.make_async_remote_copy(
            src_ref=fg_part.at[slot],
            dst_ref=fg_recv.at[slot],
            send_sem=fg_send_sem.at[slot],
            recv_sem=fg_recv_sem.at[slot],
            device_id={"rep": peer},
            device_id_type=MESH,
        )

    def filter_grad(chan):
        ats = (chan, chan + 4)
        total_r = total_i = None
        for at, spec in zip(ats, spectra(ats), strict=True):
            grad = grad_spec[at]
            sr, si, gr, gi = spec[:, :128], spec[:, 128:], grad[:, :128], grad[:, 128:]
            real, imag = sr * gr + si * gi, sr * gi - si * gr
            total_r = real if total_r is None else total_r + real
            total_i = imag if total_i is None else total_i + imag
        (part,) = inverse(tab, tw, [jnp.concatenate([total_r, total_i], 1)])
        return part

    def filter_grads(step, _):
        chan = jnp.where(step // 2 == 0, 2 * (1 - high_y), 2 * high_y)
        chan = chan + jnp.where(lax.rem(step, 2) == 0, 1 - core, core)
        fg_part[step] = filter_grad(chan)

        @pl.when(lax.rem(step, 2) == 0)
        def _():
            part_copy(step, near).start()

        @pl.when(step == 1)
        def _():
            part_copy(0, near).wait()
            fg_part[1] += fg_recv[0]
            part_copy(1, far).start()

        return 0

    lax.fori_loop(0, REP, filter_grads, 0)
    part_copy(1, far).wait()
    part_copy(2, near).wait()
    total = fg_part[3] + fg_recv[2] + fg_recv[1]
    total = total * (1.0 / 512.0)
    for half in range(2):
        for high in range(2):
            fg_out[pl.ds(2 * half + high, 64, stride=4), :] = total[
                half * 64 : half * 64 + 64, high * 128 : high * 128 + 128
            ]

    wait_all(ig_recv, recv_sem, 2)

    def finish(at, _):
        block = ig_recv[pl.ds(pl.multiple_of(at * 256, 256), 256), :]
        turned = dot(tab[P3], block).astype(BF16)
        chans = pl.ds(pl.multiple_of(at * 64, 64), 64)
        for seq in range(2):
            for half in range(2):
                start = seq * 128 + half * 64
                ig_out[seq, chans, half * 256 : half * 256 + 256] = turned[start : start + 64]
        return 0

    lax.fori_loop(0, 4, finish, 0, unroll=True)
    wait_all(og_send, send_sem, 0)
    wait_all(gi_send, send_sem, 1)
    wait_all(ig_send, send_sem, 2)


def local(gated_input, out_grad, filter_taps):
    move, tables = bf16_tables()
    taps = filter_taps.reshape(4, 256, 128).transpose(1, 0, 2).reshape(1024, 128)
    hbm = pl.BlockSpec(memory_space=pltpu.HBM)
    vmem = pl.BlockSpec(memory_space=pltpu.VMEM)
    chunks = pltpu.VMEM((CTX * ROWS, 256), BF16)
    input_grad, filter_grad = pl.pallas_call(
        kernel,
        out_shape=(
            jax.ShapeDtypeStruct((2, 256, 512), BF16),
            jax.ShapeDtypeStruct((256, 128), F32),
        ),
        in_specs=[hbm] * 6,
        out_specs=(vmem, vmem),
        scratch_shapes=[
            pltpu.VMEM((2, 256, 512), BF16),
            pltpu.VMEM((2, 256, 512), BF16),
            pltpu.VMEM((1024, 128), F32),
            pltpu.VMEM((256, 256), BF16),
            pltpu.VMEM((8, 256, 256), BF16),
            pltpu.VMEM((128, 768), F32),
            chunks, chunks, chunks, chunks, chunks, chunks,
            chunks,
            pltpu.VMEM((8, 256, 256), F32),
            pltpu.VMEM((4, 256, 256), F32),
            pltpu.VMEM((4, 128, 256), F32),
            pltpu.VMEM((3, 128, 256), F32),
            pltpu.SemaphoreType.DMA((6,)),
            pltpu.SemaphoreType.DMA((3,)),
            pltpu.SemaphoreType.DMA((3,)),
            pltpu.SemaphoreType.DMA((3,)),
            pltpu.SemaphoreType.DMA((3,)),
        ],
        compiler_params=pltpu.CompilerParams(
            collective_id=0, has_side_effects=True, vmem_limit_bytes=40 * 2**20
        ),
    )(
        *(
            pltpu.with_memory_space_constraint(operand, pltpu.HBM)
            for operand in (
                out_grad, gated_input, taps,
                jnp.asarray(move), jnp.asarray(tables), jnp.asarray(f32_tables()),
            )
        )
    )
    return input_grad, filter_grad.reshape(1, 32768)


def solution(mesh):
    return jax.shard_map(
        local,
        mesh=mesh,
        in_specs=(P("rep", None, "ctx"), P("rep", None, "ctx"), P("ctx", None)),
        out_specs=(P("rep", None, "ctx"), P(("ctx", "rep"), None)),
        check_vma=False,
    )
```

```python
import functools
import math

import jax
import jax.numpy as jnp
import ml_dtypes
import numpy as np
from jax import lax
from jax.experimental import pallas as pl
from jax.experimental.pallas import tpu as pltpu
from jax.sharding import PartitionSpec as P

MESH = pl.DeviceIdType.MESH
CTX = 64
REP = 4
ROWS = 16
F32 = jnp.float32
BF16 = jnp.bfloat16

P2, A2, DHI, DLO, EHI, ELO, BB = range(7)


def split16(table):
    high = table.astype(ml_dtypes.bfloat16)
    low = (table - high.astype(np.float64)).astype(ml_dtypes.bfloat16)
    return high, low


def bf16_tables():
    out = np.zeros((7, 256, 256), ml_dtypes.bfloat16)
    move = np.zeros((256, 256), ml_dtypes.bfloat16)
    for chan in range(64):
        for seq in range(2):
            for half in range(2):
                row = (chan // 4) * 16 + seq * 8 + (chan % 4) * 2 + half
                col = seq * 128 + half * 64 + chan
                move[row, col] = 1
    for at in range(256):
        out[P2, (at % 16) * 16 + at // 16, at] = 1
    place = np.arange(128)
    pos = 2 * (place % 64) + place // 64
    k1 = np.arange(128)
    angle = 2 * math.pi * ((pos[None, :] * (2 * k1[:, None] + 1)) % 512) / 512
    first = np.concatenate([np.cos(angle), -np.sin(angle)], 0)
    high, low = split16(first)
    out[A2] = np.concatenate([high, low], 1)
    high, low = split16(first.T * 2.0**-15)
    out[BB] = np.concatenate([high, low], 0)
    turn = 2 * math.pi * ((k1[:, None] * k1[None, :]) % 128) / 128
    cos, sin = np.cos(turn), np.sin(turn)
    out[DHI], out[DLO] = split16(np.block([[cos, -sin], [sin, cos]]))
    out[EHI], out[ELO] = split16(np.block([[cos, sin], [-sin, cos]]))
    return move, out


def pair_moves():
    out = np.zeros((2, 256, 512), ml_dtypes.bfloat16)
    for pair in range(2):
        for row in range(256):
            dest, seq, chan, half, high = row // 16, row // 8 % 2, row // 4 % 2, row // 2 % 2, row % 2
            out[pair, row, high * 256 + seq * 128 + half * 64 + dest * 4 + 2 * pair + chan] = 1
    return out


def f32_tables():
    k1 = np.arange(128)[:, None]
    q = np.arange(256)[None, :]
    angle = 2 * math.pi * (q * (2 * k1 + 1)) / 131072
    half = np.broadcast_to(2 * math.pi * np.arange(128)[None, :] / 256, (128, 128))
    return np.concatenate(
        [np.cos(angle), -np.sin(angle), np.cos(half), -np.sin(half)], 1
    ).astype(np.float32)


def dot(left, right):
    return jnp.dot(left, right, preferred_element_type=F32)


def halves(value):
    high = value.astype(BF16)
    return high, (value - high.astype(F32)).astype(BF16)


def cmul(ar, ai, br, bi):
    return ar * br - ai * bi, ar * bi + ai * br


def twiddles(tw):
    return (
        (tw[:, 0:128], tw[:, 256:384]),
        (tw[:, 128:256], tw[:, 384:512]),
        (tw[:, 512:640], tw[:, 640:768]),
    )


def transform(rows, table_high, table_low):
    count = rows.shape[0]
    high, low = halves(rows)
    wide = dot(jnp.concatenate([high, low], 0), table_high)
    return wide[:count] + wide[count:] + dot(high, table_low)


def forward(tab, tw, step, count):
    (t0r, t0i), (t1r, t1i), (wr, wi) = twiddles(tw)
    rows = []
    for at in range(count):
        lanes = 256 * at
        z0r, z0i = cmul(step[:128, lanes : lanes + 128], step[128:, lanes : lanes + 128], t0r, t0i)
        z1r, z1i = cmul(step[:128, lanes + 128 : lanes + 256], step[128:, lanes + 128 : lanes + 256], t1r, t1i)
        odd_r, odd_i = cmul(z0r - z1r, z0i - z1i, wr, wi)
        rows.append(jnp.concatenate([z0r + z1r, z0i + z1i], 1))
        rows.append(jnp.concatenate([odd_r, odd_i], 1))
    spec = transform(jnp.concatenate(rows, 0), tab[DHI], tab[DLO])
    return [spec[256 * at : 256 * at + 256] for at in range(count)]


def inverse(tab, tw, specs):
    (t0r, t0i), (t1r, t1i), (wr, wi) = twiddles(tw)
    back = transform(jnp.concatenate(specs, 0), tab[EHI], tab[ELO])
    columns = []
    for at in range(len(specs)):
        even = back[256 * at : 256 * at + 128]
        odd = back[256 * at + 128 : 256 * at + 256]
        er, ei = even[:, :128], even[:, 128:]
        dr, di = cmul(odd[:, :128], odd[:, 128:], wr, -wi)
        a0r, a0i = cmul(er + dr, ei + di, t0r, -t0i)
        a1r, a1i = cmul(er - dr, ei - di, t1r, -t1i)
        columns.append(
            jnp.concatenate(
                [jnp.concatenate([a0r, a1r], 1), jnp.concatenate([a0i, a1i], 1)], 0
            )
        )
    high, low = halves(jnp.concatenate(columns, 1))
    wide = dot(tab[BB], high)
    out = wide[:128] + wide[128:] + dot(tab[BB, :128, :], low)
    return [out[:, 256 * at : 256 * at + 256] for at in range(len(specs))]


def kernel(
    og_hbm, gi_hbm, flt_hbm, move_hbm, pair_hbm, tab_hbm, tw_hbm,
    ig_recv, fg_total,
    og_in, gi_in, flt, move, pair_move, tab, tw,
    og_send, gi_send0, gi_send1, ig_send, og_recv, gi_recv0, gi_recv1,
    rows, grad_spec, flt_spec, fg_part, fg_recv,
    in_sem, send_sem, recv_sem, fg_send_sem, fg_recv_sem,
):
    me = lax.axis_index("ctx")
    rep = lax.axis_index("rep")

    loads = [
        pltpu.make_async_copy(src, dst, in_sem.at[at])
        for at, (src, dst) in enumerate(
            ((move_hbm, move), (og_hbm, og_in), (gi_hbm, gi_in), (pair_hbm, pair_move), (flt_hbm, flt), (tab_hbm, tab), (tw_hbm, tw))
        )
    ]
    for load in loads:
        load.start()

    barrier = pltpu.get_barrier_semaphore()

    def greet(step, _):
        pl.semaphore_signal(
            barrier, inc=1, device_id={"ctx": lax.rem(me + step, CTX)}, device_id_type=MESH
        )
        return 0

    lax.fori_loop(1, CTX, greet, 0, unroll=7)
    core, high_y = lax.rem(rep, 2), rep // 2
    near = 2 * high_y + 1 - core
    far = 2 * (1 - high_y) + core
    for peer in (near, far):
        pl.semaphore_signal(barrier, inc=1, device_id={"rep": peer}, device_id_type=MESH)

    def gather(source, at):
        return jnp.concatenate(
            [
                source[seq, 64 * at : 64 * at + 64, half * 256 : half * 256 + 256]
                for seq in range(2)
                for half in range(2)
            ],
            0,
        )

    mine = pl.ds(pl.multiple_of(me * ROWS, ROWS), ROWS)

    def send_all(source, target, which):
        def send(step, _):
            away = jnp.where(step % 2 == 1, (step + 1) // 2, CTX - step // 2)
            to = lax.rem(me + away, CTX)
            pltpu.make_async_remote_copy(
                src_ref=source.at[pl.ds(pl.multiple_of(to * ROWS, ROWS), ROWS), :],
                dst_ref=target.at[mine, :],
                send_sem=send_sem.at[which],
                recv_sem=recv_sem.at[which],
                device_id={"ctx": to},
                device_id_type=MESH,
            ).start()
            return 0

        lax.fori_loop(1, CTX, send, 0, unroll=7)

    def keep_own(source, target):
        target[mine, :] = source[mine, :]

    def wait_all(buffer, sems, which):
        part = buffer.at[pl.ds(0, (CTX - 1) * ROWS), :]
        pltpu.make_async_copy(part, part, sems.at[which]).wait()

    loads[0].wait()
    loads[1].wait()
    for at in range(4):
        og_send[256 * at : 256 * at + 256, :] = dot(move[...], gather(og_in, at)).astype(BF16)
    pl.semaphore_wait(barrier, CTX - 1 + 2)
    send_all(og_send, og_recv, 0)
    keep_own(og_send, og_recv)
    loads[2].wait()
    loads[3].wait()
    pairs = ((gi_send0, gi_recv0, 1 - high_y), (gi_send1, gi_recv1, high_y))
    for which, (source, target, pair) in enumerate(pairs):
        for at in range(4):
            block = gather(gi_in, at)
            block = jnp.concatenate([block[:, :128], block[:, 128:]], 0)
            source[256 * at : 256 * at + 256, :] = dot(pair_move[pair], block).astype(BF16)
        send_all(source, target, 1 + which)
        keep_own(source, target)
    loads[4].wait()
    loads[5].wait()
    loads[6].wait()

    def filter_spectrum(chan, _):
        taps = jnp.concatenate(
            [
                jnp.concatenate(
                    [flt[pl.ds(8 * half + 4 * high + chan, 64, stride=16), :] for high in range(2)], 1
                )
                for half in range(2)
            ],
            0,
        )
        high, low = halves(taps)
        step = dot(tab[A2], jnp.concatenate([high, high], 0)) + dot(tab[A2, :, :128], low)
        (flt_spec[chan],) = forward(tab, tw, step, 1)
        return 0

    lax.fori_loop(0, 4, filter_spectrum, 0)

    def to_rows(buffer):
        for at in range(4):
            turned = dot(tab[P2], buffer[256 * at : 256 * at + 256, :]).astype(BF16)
            for row in range(16):
                start = row * 64 + at * 16
                rows[start : start + 16, :] = turned[row * 16 : row * 16 + 16]

    def pair_to_rows(buffer, pair):
        for at in range(4):
            turned = dot(tab[P2], buffer[256 * at : 256 * at + 256, :]).astype(BF16)
            for row in range(16):
                seq, chan, half, high = row // 8, row // 4 % 2, row // 2 % 2, row % 2
                start = pair * 256 + seq * 512 + chan * 128 + half * 64 + at * 16
                rows[pl.ds(pl.multiple_of(start, 16), 16), 128 * high : 128 * high + 128] = turned[
                    row * 16 : row * 16 + 16
                ]

    def spectra(ats):
        blocks = jnp.concatenate(
            [rows[pl.ds(pl.multiple_of(at * 128, 128), 128), :] for at in ats], 1
        )
        step = dot(tab[A2], jnp.concatenate([blocks, blocks], 0))
        return forward(tab, tw, step, len(ats))

    wait_all(og_recv, recv_sem, 0)
    to_rows(og_recv)

    def input_grad(chan, _):
        ats = (chan, chan + 4)
        taps = flt_spec[chan]
        fr, fi = taps[:, :128], taps[:, 128:]
        specs = spectra(ats)
        corrs = []
        for spec in specs:
            sr, si = spec[:, :128], spec[:, 128:]
            corrs.append(jnp.concatenate([fr * sr + fi * si, fr * si - fi * sr], 1))
        grads = inverse(tab, tw, corrs)
        for at, spec, grad in zip(ats, specs, grads, strict=True):
            grad_spec[at] = spec
            rows[pl.ds(pl.multiple_of(at * 128, 128), 128), :] = grad.astype(BF16)
        return 0

    lax.fori_loop(0, 4, input_grad, 0)

    def from_rows(at, _):
        block = jnp.concatenate(
            [rows[pl.ds(pl.multiple_of(row * 64 + at * 16, 16), 16), :] for row in range(16)], 0
        )
        ig_send[pl.ds(pl.multiple_of(at * 256, 256), 256), :] = dot(tab[P2], block).astype(BF16)
        return 0

    lax.fori_loop(0, 4, from_rows, 0, unroll=True)
    send_all(ig_send, ig_recv, 3)
    keep_own(ig_send, ig_recv)

    def part_copy(slot, peer):
        return pltpu.make_async_remote_copy(
            src_ref=fg_part.at[slot],
            dst_ref=fg_recv.at[slot],
            send_sem=fg_send_sem.at[slot],
            recv_sem=fg_recv_sem.at[slot],
            device_id={"rep": peer},
            device_id_type=MESH,
        )

    def filter_grad(chan):
        ats = (chan, chan + 4)
        total_r = total_i = None
        for at, spec in zip(ats, spectra(ats), strict=True):
            grad = grad_spec[at]
            sr, si, gr, gi = spec[:, :128], spec[:, 128:], grad[:, :128], grad[:, 128:]
            real, imag = sr * gr + si * gi, sr * gi - si * gr
            total_r = real if total_r is None else total_r + real
            total_i = imag if total_i is None else total_i + imag
        (part,) = inverse(tab, tw, [jnp.concatenate([total_r, total_i], 1)])
        return part

    for which, (_, target, pair) in enumerate(pairs):
        wait_all(target, recv_sem, 1 + which)
        pair_to_rows(target, pair)

        def filter_grads(step, _):
            chan = 2 * pair + jnp.where(step == 0, 1 - core, core)
            fg_part[2 * which + step] = filter_grad(chan)

            @pl.when(step == 0)
            def _():
                part_copy(2 * which, near).start()

            return 0

        lax.fori_loop(0, 2, filter_grads, 0)
        if which == 0:
            part_copy(0, near).wait()
            fg_part[1] += fg_recv[0]
            part_copy(1, far).start()
    part_copy(1, far).wait()
    part_copy(2, near).wait()
    total = fg_part[3] + fg_recv[2] + fg_recv[1]
    fg_total[...] = total
    wait_all(ig_recv, recv_sem, 3)
    wait_all(og_send, send_sem, 0)
    wait_all(gi_send0, send_sem, 1)
    wait_all(gi_send1, send_sem, 2)
    wait_all(ig_send, send_sem, 3)


def finish(chunk_rows, total, ig_hbm, fg_hbm, ig_out, fg_out, sem):
    scaled = total[...] * (1.0 / 512.0)
    for half in range(2):
        for high in range(2):
            fg_out[pl.ds(2 * half + high, 64, stride=4), :] = scaled[
                half * 64 : half * 64 + 64, high * 128 : high * 128 + 128
            ]
    copies = [pltpu.make_async_copy(fg_out, fg_hbm, sem.at[4])]
    copies[0].start()
    row = lax.broadcasted_iota(jnp.int32, (256, 256), 0)
    col = lax.broadcasted_iota(jnp.int32, (256, 256), 1)
    chan = row % 64
    source = chan // 4 * 16 + row // 128 * 8 + chan % 4 * 2 + row // 64 % 2
    move = jnp.where(source == col, 1.0, 0.0).astype(BF16)
    for at in range(4):
        turned = dot(move, chunk_rows[256 * at : 256 * at + 256, :]).astype(BF16)
        chans = pl.ds(64 * at, 64)
        for seq in range(2):
            for half in range(2):
                start = seq * 128 + half * 64
                ig_out[seq, chans, half * 256 : half * 256 + 256] = turned[start : start + 64]
        copies.append(
            pltpu.make_async_copy(ig_out.at[:, chans, :], ig_hbm.at[:, chans, :], sem.at[at])
        )
        copies[-1].start()
    for copy in copies:
        copy.wait()


def local(gated_input, out_grad, filter_taps):
    move, tables = bf16_tables()
    taps = filter_taps.reshape(4, 256, 128).transpose(1, 0, 2).reshape(1024, 128)
    hbm = pl.BlockSpec(memory_space=pltpu.HBM)
    vmem = pl.BlockSpec(memory_space=pltpu.VMEM)
    chunks = pltpu.VMEM((CTX * ROWS, 256), BF16)
    pair_chunks = pltpu.VMEM((CTX * ROWS, 128), BF16)
    chunk_rows, total = pl.pallas_call(
        kernel,
        out_shape=(
            jax.ShapeDtypeStruct((CTX * ROWS, 256), BF16),
            jax.ShapeDtypeStruct((128, 256), F32),
        ),
        in_specs=[hbm] * 7,
        out_specs=(vmem, vmem),
        scratch_shapes=[
            pltpu.VMEM((2, 256, 512), BF16),
            pltpu.VMEM((2, 256, 512), BF16),
            pltpu.VMEM((1024, 128), F32),
            pltpu.VMEM((256, 256), BF16),
            pltpu.VMEM((2, 256, 512), BF16),
            pltpu.VMEM((7, 256, 256), BF16),
            pltpu.VMEM((128, 768), F32),
            chunks, pair_chunks, pair_chunks, chunks, chunks, pair_chunks, pair_chunks,
            chunks,
            pltpu.VMEM((8, 256, 256), F32),
            pltpu.VMEM((4, 256, 256), F32),
            pltpu.VMEM((4, 128, 256), F32),
            pltpu.VMEM((3, 128, 256), F32),
            pltpu.SemaphoreType.DMA((7,)),
            pltpu.SemaphoreType.DMA((4,)),
            pltpu.SemaphoreType.DMA((4,)),
            pltpu.SemaphoreType.DMA((3,)),
            pltpu.SemaphoreType.DMA((3,)),
        ],
        compiler_params=pltpu.CompilerParams(
            collective_id=0, has_side_effects=True, vmem_limit_bytes=40 * 2**20
        ),
    )(
        *(
            pltpu.with_memory_space_constraint(operand, pltpu.HBM)
            for operand in (
                out_grad, gated_input, taps,
                jnp.asarray(move), jnp.asarray(pair_moves()), jnp.asarray(tables), jnp.asarray(f32_tables()),
            )
        )
    )
    input_grad, filter_grad = pl.pallas_call(
        finish,
        out_shape=(
            jax.ShapeDtypeStruct((2, 256, 512), BF16),
            jax.ShapeDtypeStruct((256, 128), F32),
        ),
        in_specs=[vmem, vmem],
        out_specs=(pl.BlockSpec(memory_space=pl.ANY),) * 2,
        scratch_shapes=[
            pltpu.VMEM((2, 256, 512), BF16),
            pltpu.VMEM((256, 128), F32),
            pltpu.SemaphoreType.DMA((5,)),
        ],
        compiler_params=pltpu.CompilerParams(vmem_limit_bytes=16 * 2**20),
    )(chunk_rows, total)
    return input_grad, filter_grad.reshape(1, 32768)


def solution(mesh):
    return jax.shard_map(
        local,
        mesh=mesh,
        in_specs=(P("rep", None, "ctx"), P("rep", None, "ctx"), P("ctx", None)),
        out_specs=(P("rep", None, "ctx"), P(("ctx", "rep"), None)),
        check_vma=False,
    )
```

```python
import functools
import math

import jax
import jax.numpy as jnp
import ml_dtypes
import numpy as np
from jax import lax
from jax.experimental import pallas as pl
from jax.experimental.pallas import tpu as pltpu
from jax.sharding import PartitionSpec as P

MESH = pl.DeviceIdType.MESH
CTX = 64
REP = 4
ROWS = 16
F32 = jnp.float32
BF16 = jnp.bfloat16

P2, A2, DHI, DLO, EHI, ELO, BB = range(7)


def split16(table):
    high = table.astype(ml_dtypes.bfloat16)
    low = (table - high.astype(np.float64)).astype(ml_dtypes.bfloat16)
    return high, low


def bf16_tables():
    out = np.zeros((7, 256, 256), ml_dtypes.bfloat16)
    move = np.zeros((256, 256), ml_dtypes.bfloat16)
    for chan in range(64):
        for seq in range(2):
            for half in range(2):
                row = (chan // 4) * 16 + seq * 8 + (chan % 4) * 2 + half
                col = seq * 128 + half * 64 + chan
                move[row, col] = 1
    for at in range(256):
        out[P2, (at % 16) * 16 + at // 16, at] = 1
    place = np.arange(128)
    pos = 2 * (place % 64) + place // 64
    k1 = np.arange(128)
    angle = 2 * math.pi * ((pos[None, :] * (2 * k1[:, None] + 1)) % 512) / 512
    first = np.concatenate([np.cos(angle), -np.sin(angle)], 0)
    high, low = split16(first)
    out[A2] = np.concatenate([high, low], 1)
    high, low = split16(first.T * 2.0**-15)
    out[BB] = np.concatenate([high, low], 0)
    turn = 2 * math.pi * ((k1[:, None] * k1[None, :]) % 128) / 128
    cos, sin = np.cos(turn), np.sin(turn)
    out[DHI], out[DLO] = split16(np.block([[cos, -sin], [sin, cos]]))
    out[EHI], out[ELO] = split16(np.block([[cos, sin], [-sin, cos]]))
    return move, out


def pair_moves():
    out = np.zeros((2, 256, 512), ml_dtypes.bfloat16)
    for pair in range(2):
        for row in range(256):
            dest, seq, chan, half, high = row // 16, row // 8 % 2, row // 4 % 2, row // 2 % 2, row % 2
            out[pair, row, high * 256 + seq * 128 + half * 64 + dest * 4 + 2 * pair + chan] = 1
    return out


def f32_tables():
    k1 = np.arange(128)[:, None]
    q = np.arange(256)[None, :]
    angle = 2 * math.pi * (q * (2 * k1 + 1)) / 131072
    half = np.broadcast_to(2 * math.pi * np.arange(128)[None, :] / 256, (128, 128))
    return np.concatenate(
        [np.cos(angle), -np.sin(angle), np.cos(half), -np.sin(half)], 1
    ).astype(np.float32)


def dot(left, right):
    return jnp.dot(left, right, preferred_element_type=F32)


def halves(value):
    high = value.astype(BF16)
    return high, (value - high.astype(F32)).astype(BF16)


def cmul(ar, ai, br, bi):
    return ar * br - ai * bi, ar * bi + ai * br


def twiddles(tw):
    return (
        (tw[:, 0:128], tw[:, 256:384]),
        (tw[:, 128:256], tw[:, 384:512]),
        (tw[:, 512:640], tw[:, 640:768]),
    )


def transform(rows, table_high, table_low):
    count = rows.shape[0]
    high, low = halves(rows)
    wide = dot(jnp.concatenate([high, low], 0), table_high)
    return wide[:count] + wide[count:] + dot(high, table_low)


def forward(tab, tw, step, count):
    (t0r, t0i), (t1r, t1i), (wr, wi) = twiddles(tw)
    rows = []
    for at in range(count):
        lanes = 256 * at
        z0r, z0i = cmul(step[:128, lanes : lanes + 128], step[128:, lanes : lanes + 128], t0r, t0i)
        z1r, z1i = cmul(step[:128, lanes + 128 : lanes + 256], step[128:, lanes + 128 : lanes + 256], t1r, t1i)
        odd_r, odd_i = cmul(z0r - z1r, z0i - z1i, wr, wi)
        rows.append(jnp.concatenate([z0r + z1r, z0i + z1i], 1))
        rows.append(jnp.concatenate([odd_r, odd_i], 1))
    spec = transform(jnp.concatenate(rows, 0), tab[DHI], tab[DLO])
    return [spec[256 * at : 256 * at + 256] for at in range(count)]


def inverse(tab, tw, specs):
    (t0r, t0i), (t1r, t1i), (wr, wi) = twiddles(tw)
    back = transform(jnp.concatenate(specs, 0), tab[EHI], tab[ELO])
    columns = []
    for at in range(len(specs)):
        even = back[256 * at : 256 * at + 128]
        odd = back[256 * at + 128 : 256 * at + 256]
        er, ei = even[:, :128], even[:, 128:]
        dr, di = cmul(odd[:, :128], odd[:, 128:], wr, -wi)
        a0r, a0i = cmul(er + dr, ei + di, t0r, -t0i)
        a1r, a1i = cmul(er - dr, ei - di, t1r, -t1i)
        columns.append(
            jnp.concatenate(
                [jnp.concatenate([a0r, a1r], 1), jnp.concatenate([a0i, a1i], 1)], 0
            )
        )
    high, low = halves(jnp.concatenate(columns, 1))
    wide = dot(tab[BB], high)
    out = wide[:128] + wide[128:] + dot(tab[BB, :128, :], low)
    return [out[:, 256 * at : 256 * at + 256] for at in range(len(specs))]


def kernel(
    og_hbm, gi_hbm, flt_hbm, move_hbm, pair_hbm, tab_hbm, tw_hbm,
    ig_recv, fg_total,
    og_in, gi_in, flt, move, pair_move, tab, tw,
    og_send, gi_send0, gi_send1, ig_send, og_recv, gi_recv0, gi_recv1,
    rows, grad_spec, flt_spec, fg_part, fg_recv,
    in_sem, send_sem, recv_sem, fg_send_sem, fg_recv_sem,
):
    me = lax.axis_index("ctx")
    rep = lax.axis_index("rep")

    loads = [
        pltpu.make_async_copy(src, dst, in_sem.at[at])
        for at, (src, dst) in enumerate(
            ((move_hbm, move), (og_hbm, og_in), (gi_hbm, gi_in), (pair_hbm, pair_move), (flt_hbm, flt), (tab_hbm, tab), (tw_hbm, tw))
        )
    ]
    for load in loads:
        load.start()

    barrier = pltpu.get_barrier_semaphore()

    def greet(step, _):
        away = jnp.where(step % 2 == 1, 32 - step // 2, 32 + step // 2)
        pl.semaphore_signal(
            barrier, inc=1, device_id={"ctx": lax.rem(me + away, CTX)}, device_id_type=MESH
        )
        return 0

    lax.fori_loop(1, CTX, greet, 0, unroll=21)
    core, high_y = lax.rem(rep, 2), rep // 2
    near = 2 * high_y + 1 - core
    far = 2 * (1 - high_y) + core
    for peer in (near, far):
        pl.semaphore_signal(barrier, inc=1, device_id={"rep": peer}, device_id_type=MESH)

    def gather(source, at):
        return jnp.concatenate(
            [
                source[seq, 64 * at : 64 * at + 64, half * 256 : half * 256 + 256]
                for seq in range(2)
                for half in range(2)
            ],
            0,
        )

    mine = pl.ds(pl.multiple_of(me * ROWS, ROWS), ROWS)

    def send_all(source, target, which):
        def send(step, _):
            away = jnp.where(step % 2 == 1, (step + 1) // 2, CTX - step // 2)
            to = lax.rem(me + away, CTX)
            pltpu.make_async_remote_copy(
                src_ref=source.at[pl.ds(pl.multiple_of(to * ROWS, ROWS), ROWS), :],
                dst_ref=target.at[mine, :],
                send_sem=send_sem.at[which],
                recv_sem=recv_sem.at[which],
                device_id={"ctx": to},
                device_id_type=MESH,
            ).start()
            return 0

        lax.fori_loop(1, CTX, send, 0, unroll=7)

    def keep_own(source, target):
        target[mine, :] = source[mine, :]

    def wait_all(buffer, sems, which):
        part = buffer.at[pl.ds(0, (CTX - 1) * ROWS), :]
        pltpu.make_async_copy(part, part, sems.at[which]).wait()

    loads[0].wait()
    loads[1].wait()
    for at in range(4):
        og_send[256 * at : 256 * at + 256, :] = dot(move[...], gather(og_in, at)).astype(BF16)
    pl.semaphore_wait(barrier, CTX - 1 + 2)
    send_all(og_send, og_recv, 0)
    keep_own(og_send, og_recv)
    loads[2].wait()
    loads[3].wait()
    pairs = ((gi_send0, gi_recv0, 1 - high_y), (gi_send1, gi_recv1, high_y))
    for which, (source, target, pair) in enumerate(pairs):
        for at in range(4):
            block = gather(gi_in, at)
            block = jnp.concatenate([block[:, :128], block[:, 128:]], 0)
            source[256 * at : 256 * at + 256, :] = dot(pair_move[pair], block).astype(BF16)
        send_all(source, target, 1 + which)
        keep_own(source, target)
    loads[4].wait()
    loads[5].wait()
    loads[6].wait()

    def filter_spectrum(chan, _):
        taps = jnp.concatenate(
            [
                jnp.concatenate(
                    [flt[pl.ds(8 * half + 4 * high + chan, 64, stride=16), :] for high in range(2)], 1
                )
                for half in range(2)
            ],
            0,
        )
        high, low = halves(taps)
        step = dot(tab[A2], jnp.concatenate([high, high], 0)) + dot(tab[A2, :, :128], low)
        (flt_spec[chan],) = forward(tab, tw, step, 1)
        return 0

    lax.fori_loop(0, 4, filter_spectrum, 0)

    def to_rows(buffer):
        for at in range(4):
            turned = dot(tab[P2], buffer[256 * at : 256 * at + 256, :]).astype(BF16)
            for row in range(16):
                start = row * 64 + at * 16
                rows[start : start + 16, :] = turned[row * 16 : row * 16 + 16]

    def pair_to_rows(buffer, pair):
        for at in range(4):
            turned = dot(tab[P2], buffer[256 * at : 256 * at + 256, :]).astype(BF16)
            for row in range(16):
                seq, chan, half, high = row // 8, row // 4 % 2, row // 2 % 2, row % 2
                start = pair * 256 + seq * 512 + chan * 128 + half * 64 + at * 16
                rows[pl.ds(pl.multiple_of(start, 16), 16), 128 * high : 128 * high + 128] = turned[
                    row * 16 : row * 16 + 16
                ]

    def spectra(ats):
        blocks = jnp.concatenate(
            [rows[pl.ds(pl.multiple_of(at * 128, 128), 128), :] for at in ats], 1
        )
        step = dot(tab[A2], jnp.concatenate([blocks, blocks], 0))
        return forward(tab, tw, step, len(ats))

    wait_all(og_recv, recv_sem, 0)
    to_rows(og_recv)

    def input_grad(chan, _):
        ats = (chan, chan + 4)
        taps = flt_spec[chan]
        fr, fi = taps[:, :128], taps[:, 128:]
        specs = spectra(ats)
        corrs = []
        for spec in specs:
            sr, si = spec[:, :128], spec[:, 128:]
            corrs.append(jnp.concatenate([fr * sr + fi * si, fr * si - fi * sr], 1))
        grads = inverse(tab, tw, corrs)
        for at, spec, grad in zip(ats, specs, grads, strict=True):
            grad_spec[at] = spec
            rows[pl.ds(pl.multiple_of(at * 128, 128), 128), :] = grad.astype(BF16)
        return 0

    lax.fori_loop(0, 4, input_grad, 0)

    def from_rows(at, _):
        block = jnp.concatenate(
            [rows[pl.ds(pl.multiple_of(row * 64 + at * 16, 16), 16), :] for row in range(16)], 0
        )
        ig_send[pl.ds(pl.multiple_of(at * 256, 256), 256), :] = dot(tab[P2], block).astype(BF16)
        return 0

    lax.fori_loop(0, 4, from_rows, 0, unroll=True)
    send_all(ig_send, ig_recv, 3)
    keep_own(ig_send, ig_recv)

    def part_copy(slot, peer):
        return pltpu.make_async_remote_copy(
            src_ref=fg_part.at[slot],
            dst_ref=fg_recv.at[slot],
            send_sem=fg_send_sem.at[slot],
            recv_sem=fg_recv_sem.at[slot],
            device_id={"rep": peer},
            device_id_type=MESH,
        )

    def filter_grad(chan):
        ats = (chan, chan + 4)
        total_r = total_i = None
        for at, spec in zip(ats, spectra(ats), strict=True):
            grad = grad_spec[at]
            sr, si, gr, gi = spec[:, :128], spec[:, 128:], grad[:, :128], grad[:, 128:]
            real, imag = sr * gr + si * gi, sr * gi - si * gr
            total_r = real if total_r is None else total_r + real
            total_i = imag if total_i is None else total_i + imag
        (part,) = inverse(tab, tw, [jnp.concatenate([total_r, total_i], 1)])
        return part

    for which, (_, target, pair) in enumerate(pairs):
        wait_all(target, recv_sem, 1 + which)
        pair_to_rows(target, pair)

        def filter_grads(step, _):
            chan = 2 * pair + jnp.where(step == 0, 1 - core, core)
            fg_part[2 * which + step] = filter_grad(chan)

            @pl.when(step == 0)
            def _():
                part_copy(2 * which, near).start()

            return 0

        lax.fori_loop(0, 2, filter_grads, 0)
        if which == 0:
            part_copy(0, near).wait()
            fg_part[1] += fg_recv[0]
            part_copy(1, far).start()
    part_copy(1, far).wait()
    part_copy(2, near).wait()
    total = fg_part[3] + fg_recv[2] + fg_recv[1]
    fg_total[...] = total
    wait_all(ig_recv, recv_sem, 3)
    wait_all(og_send, send_sem, 0)
    wait_all(gi_send0, send_sem, 1)
    wait_all(gi_send1, send_sem, 2)
    wait_all(ig_send, send_sem, 3)


def finish(chunk_rows, total, ig_hbm, fg_hbm, ig_out, fg_out, sem):
    scaled = total[...] * (1.0 / 512.0)
    for half in range(2):
        for high in range(2):
            fg_out[pl.ds(2 * half + high, 64, stride=4), :] = scaled[
                half * 64 : half * 64 + 64, high * 128 : high * 128 + 128
            ]
    copies = [pltpu.make_async_copy(fg_out, fg_hbm, sem.at[4])]
    copies[0].start()
    row = lax.broadcasted_iota(jnp.int32, (256, 256), 0)
    col = lax.broadcasted_iota(jnp.int32, (256, 256), 1)
    chan = row % 64
    source = chan // 4 * 16 + row // 128 * 8 + chan % 4 * 2 + row // 64 % 2
    move = jnp.where(source == col, 1.0, 0.0).astype(BF16)
    for at in range(4):
        turned = dot(move, chunk_rows[256 * at : 256 * at + 256, :]).astype(BF16)
        chans = pl.ds(64 * at, 64)
        for seq in range(2):
            for half in range(2):
                start = seq * 128 + half * 64
                ig_out[seq, chans, half * 256 : half * 256 + 256] = turned[start : start + 64]
        copies.append(
            pltpu.make_async_copy(ig_out.at[:, chans, :], ig_hbm.at[:, chans, :], sem.at[at])
        )
        copies[-1].start()
    for copy in copies:
        copy.wait()


def local(gated_input, out_grad, filter_taps):
    move, tables = bf16_tables()
    taps = filter_taps.reshape(4, 256, 128).transpose(1, 0, 2).reshape(1024, 128)
    hbm = pl.BlockSpec(memory_space=pltpu.HBM)
    vmem = pl.BlockSpec(memory_space=pltpu.VMEM)
    chunks = pltpu.VMEM((CTX * ROWS, 256), BF16)
    pair_chunks = pltpu.VMEM((CTX * ROWS, 128), BF16)
    chunk_rows, total = pl.pallas_call(
        kernel,
        out_shape=(
            jax.ShapeDtypeStruct((CTX * ROWS, 256), BF16),
            jax.ShapeDtypeStruct((128, 256), F32),
        ),
        in_specs=[hbm] * 7,
        out_specs=(vmem, vmem),
        scratch_shapes=[
            pltpu.VMEM((2, 256, 512), BF16),
            pltpu.VMEM((2, 256, 512), BF16),
            pltpu.VMEM((1024, 128), F32),
            pltpu.VMEM((256, 256), BF16),
            pltpu.VMEM((2, 256, 512), BF16),
            pltpu.VMEM((7, 256, 256), BF16),
            pltpu.VMEM((128, 768), F32),
            chunks, pair_chunks, pair_chunks, chunks, chunks, pair_chunks, pair_chunks,
            chunks,
            pltpu.VMEM((8, 256, 256), F32),
            pltpu.VMEM((4, 256, 256), F32),
            pltpu.VMEM((4, 128, 256), F32),
            pltpu.VMEM((3, 128, 256), F32),
            pltpu.SemaphoreType.DMA((7,)),
            pltpu.SemaphoreType.DMA((4,)),
            pltpu.SemaphoreType.DMA((4,)),
            pltpu.SemaphoreType.DMA((3,)),
            pltpu.SemaphoreType.DMA((3,)),
        ],
        compiler_params=pltpu.CompilerParams(
            collective_id=0, has_side_effects=True, vmem_limit_bytes=40 * 2**20
        ),
    )(
        *(
            pltpu.with_memory_space_constraint(operand, pltpu.HBM)
            for operand in (
                out_grad, gated_input, taps,
                jnp.asarray(move), jnp.asarray(pair_moves()), jnp.asarray(tables), jnp.asarray(f32_tables()),
            )
        )
    )
    input_grad, filter_grad = pl.pallas_call(
        finish,
        out_shape=(
            jax.ShapeDtypeStruct((2, 256, 512), BF16),
            jax.ShapeDtypeStruct((256, 128), F32),
        ),
        in_specs=[vmem, vmem],
        out_specs=(pl.BlockSpec(memory_space=pl.ANY),) * 2,
        scratch_shapes=[
            pltpu.VMEM((2, 256, 512), BF16),
            pltpu.VMEM((256, 128), F32),
            pltpu.SemaphoreType.DMA((5,)),
        ],
        compiler_params=pltpu.CompilerParams(vmem_limit_bytes=16 * 2**20),
    )(chunk_rows, total)
    return input_grad, filter_grad.reshape(1, 32768)


def solution(mesh):
    return jax.shard_map(
        local,
        mesh=mesh,
        in_specs=(P("rep", None, "ctx"), P("rep", None, "ctx"), P("ctx", None)),
        out_specs=(P("rep", None, "ctx"), P(("ctx", "rep"), None)),
        check_vma=False,
    )
```

```python
import functools
import math

import jax
import jax.numpy as jnp
import ml_dtypes
import numpy as np
from jax import lax
from jax.experimental import pallas as pl
from jax.experimental.pallas import tpu as pltpu
from jax.sharding import PartitionSpec as P

MESH = pl.DeviceIdType.MESH
CTX = 64
REP = 4
ROWS = 16
F32 = jnp.float32
BF16 = jnp.bfloat16

P2, A2, DHI, DLO, EHI, ELO, BB = range(7)


def split16(table):
    high = table.astype(ml_dtypes.bfloat16)
    low = (table - high.astype(np.float64)).astype(ml_dtypes.bfloat16)
    return high, low


def bf16_tables():
    out = np.zeros((7, 256, 256), ml_dtypes.bfloat16)
    move = np.zeros((256, 256), ml_dtypes.bfloat16)
    for chan in range(64):
        for seq in range(2):
            for half in range(2):
                row = (chan // 4) * 16 + seq * 8 + (chan % 4) * 2 + half
                col = seq * 128 + half * 64 + chan
                move[row, col] = 1
    for at in range(256):
        out[P2, (at % 16) * 16 + at // 16, at] = 1
    place = np.arange(128)
    pos = 2 * (place % 64) + place // 64
    k1 = np.arange(128)
    angle = 2 * math.pi * ((pos[None, :] * (2 * k1[:, None] + 1)) % 512) / 512
    first = np.concatenate([np.cos(angle), -np.sin(angle)], 0)
    high, low = split16(first)
    out[A2] = np.concatenate([high, low], 1)
    high, low = split16(first.T * 2.0**-15)
    out[BB] = np.concatenate([high, low], 0)
    turn = 2 * math.pi * ((k1[:, None] * k1[None, :]) % 128) / 128
    cos, sin = np.cos(turn), np.sin(turn)
    out[DHI], out[DLO] = split16(np.block([[cos, -sin], [sin, cos]]))
    out[EHI], out[ELO] = split16(np.block([[cos, sin], [-sin, cos]]))
    return move, out


def pair_moves():
    out = np.zeros((2, 256, 512), ml_dtypes.bfloat16)
    for pair in range(2):
        for row in range(256):
            dest, seq, chan, half, high = row // 16, row // 8 % 2, row // 4 % 2, row // 2 % 2, row % 2
            out[pair, row, high * 256 + seq * 128 + half * 64 + dest * 4 + 2 * pair + chan] = 1
    return out


def f32_tables():
    k1 = np.arange(128)[:, None]
    q = np.arange(256)[None, :]
    angle = 2 * math.pi * (q * (2 * k1 + 1)) / 131072
    half = np.broadcast_to(2 * math.pi * np.arange(128)[None, :] / 256, (128, 128))
    return np.concatenate(
        [np.cos(angle), -np.sin(angle), np.cos(half), -np.sin(half)], 1
    ).astype(np.float32)


def dot(left, right):
    return jnp.dot(left, right, preferred_element_type=F32)


def halves(value):
    high = value.astype(BF16)
    return high, (value - high.astype(F32)).astype(BF16)


def cmul(ar, ai, br, bi):
    return ar * br - ai * bi, ar * bi + ai * br


def twiddles(tw):
    return (
        (tw[:, 0:128], tw[:, 256:384]),
        (tw[:, 128:256], tw[:, 384:512]),
        (tw[:, 512:640], tw[:, 640:768]),
    )


def transform(rows, table_high, table_low):
    count = rows.shape[0]
    high, low = halves(rows)
    wide = dot(jnp.concatenate([high, low], 0), table_high)
    return wide[:count] + wide[count:] + dot(high, table_low)


def forward(tab, tw, step, count):
    (t0r, t0i), (t1r, t1i), (wr, wi) = twiddles(tw)
    rows = []
    for at in range(count):
        lanes = 256 * at
        z0r, z0i = cmul(step[:128, lanes : lanes + 128], step[128:, lanes : lanes + 128], t0r, t0i)
        z1r, z1i = cmul(step[:128, lanes + 128 : lanes + 256], step[128:, lanes + 128 : lanes + 256], t1r, t1i)
        odd_r, odd_i = cmul(z0r - z1r, z0i - z1i, wr, wi)
        rows.append(jnp.concatenate([z0r + z1r, z0i + z1i], 1))
        rows.append(jnp.concatenate([odd_r, odd_i], 1))
    spec = transform(jnp.concatenate(rows, 0), tab[DHI], tab[DLO])
    return [spec[256 * at : 256 * at + 256] for at in range(count)]


def inverse(tab, tw, specs):
    (t0r, t0i), (t1r, t1i), (wr, wi) = twiddles(tw)
    back = transform(jnp.concatenate(specs, 0), tab[EHI], tab[ELO])
    columns = []
    for at in range(len(specs)):
        even = back[256 * at : 256 * at + 128]
        odd = back[256 * at + 128 : 256 * at + 256]
        er, ei = even[:, :128], even[:, 128:]
        dr, di = cmul(odd[:, :128], odd[:, 128:], wr, -wi)
        a0r, a0i = cmul(er + dr, ei + di, t0r, -t0i)
        a1r, a1i = cmul(er - dr, ei - di, t1r, -t1i)
        columns.append(
            jnp.concatenate(
                [jnp.concatenate([a0r, a1r], 1), jnp.concatenate([a0i, a1i], 1)], 0
            )
        )
    high, low = halves(jnp.concatenate(columns, 1))
    wide = dot(tab[BB], high)
    out = wide[:128] + wide[128:] + dot(tab[BB, :128, :], low)
    return [out[:, 256 * at : 256 * at + 256] for at in range(len(specs))]


def kernel(
    og_hbm, gi_hbm, flt_hbm, move_hbm, pair_hbm, tab_hbm, tw_hbm,
    ig_out, fg_out,
    og_in, gi_in, flt, move, pair_move, tab, tw,
    og_send, gi_send0, gi_send1, ig_send, og_recv, gi_recv0, gi_recv1, ig_recv,
    rows, grad_spec, flt_spec, fg_part, fg_recv,
    in_sem, send_sem, recv_sem, fg_send_sem, fg_recv_sem,
):
    me = lax.axis_index("ctx")
    rep = lax.axis_index("rep")

    loads = [
        pltpu.make_async_copy(src, dst, in_sem.at[at])
        for at, (src, dst) in enumerate(
            ((move_hbm, move), (og_hbm, og_in), (gi_hbm, gi_in), (pair_hbm, pair_move), (flt_hbm, flt), (tab_hbm, tab), (tw_hbm, tw))
        )
    ]
    for load in loads:
        load.start()

    barrier = pltpu.get_barrier_semaphore()

    def greet(step, _):
        away = jnp.where(step % 2 == 1, 32 - step // 2, 32 + step // 2)
        pl.semaphore_signal(
            barrier, inc=1, device_id={"ctx": lax.rem(me + away, CTX)}, device_id_type=MESH
        )
        return 0

    lax.fori_loop(1, CTX, greet, 0, unroll=21)
    core, high_y = lax.rem(rep, 2), rep // 2
    near = 2 * high_y + 1 - core
    far = 2 * (1 - high_y) + core
    for peer in (near, far):
        pl.semaphore_signal(barrier, inc=1, device_id={"rep": peer}, device_id_type=MESH)

    def gather(source, at):
        return jnp.concatenate(
            [
                source[seq, 64 * at : 64 * at + 64, half * 256 : half * 256 + 256]
                for seq in range(2)
                for half in range(2)
            ],
            0,
        )

    mine = pl.ds(pl.multiple_of(me * ROWS, ROWS), ROWS)

    def send_all(source, target, which):
        def send(step, _):
            away = jnp.where(step % 2 == 1, (step + 1) // 2, CTX - step // 2)
            to = lax.rem(me + away, CTX)
            pltpu.make_async_remote_copy(
                src_ref=source.at[pl.ds(pl.multiple_of(to * ROWS, ROWS), ROWS), :],
                dst_ref=target.at[mine, :],
                send_sem=send_sem.at[which],
                recv_sem=recv_sem.at[which],
                device_id={"ctx": to},
                device_id_type=MESH,
            ).start()
            return 0

        lax.fori_loop(1, CTX, send, 0, unroll=7)

    def keep_own(source, target):
        target[mine, :] = source[mine, :]

    def wait_all(buffer, sems, which):
        part = buffer.at[pl.ds(0, (CTX - 1) * ROWS), :]
        pltpu.make_async_copy(part, part, sems.at[which]).wait()

    loads[0].wait()
    loads[1].wait()
    for at in range(4):
        og_send[256 * at : 256 * at + 256, :] = dot(move[...], gather(og_in, at)).astype(BF16)
    pl.semaphore_wait(barrier, CTX - 1 + 2)
    send_all(og_send, og_recv, 0)
    keep_own(og_send, og_recv)
    loads[2].wait()
    loads[3].wait()
    pairs = ((gi_send0, gi_recv0, 1 - high_y), (gi_send1, gi_recv1, high_y))
    for which, (source, target, pair) in enumerate(pairs):
        for at in range(4):
            block = gather(gi_in, at)
            block = jnp.concatenate([block[:, :128], block[:, 128:]], 0)
            source[256 * at : 256 * at + 256, :] = dot(pair_move[pair], block).astype(BF16)
        send_all(source, target, 1 + which)
        keep_own(source, target)
    loads[4].wait()
    loads[5].wait()
    loads[6].wait()

    def filter_spectrum(chan, _):
        taps = jnp.concatenate(
            [
                jnp.concatenate(
                    [flt[pl.ds(8 * half + 4 * high + chan, 64, stride=16), :] for high in range(2)], 1
                )
                for half in range(2)
            ],
            0,
        )
        high, low = halves(taps)
        step = dot(tab[A2], jnp.concatenate([high, high], 0)) + dot(tab[A2, :, :128], low)
        (flt_spec[chan],) = forward(tab, tw, step, 1)
        return 0

    lax.fori_loop(0, 4, filter_spectrum, 0)

    def to_rows(buffer):
        for at in range(4):
            turned = dot(tab[P2], buffer[256 * at : 256 * at + 256, :]).astype(BF16)
            for row in range(16):
                start = row * 64 + at * 16
                rows[start : start + 16, :] = turned[row * 16 : row * 16 + 16]

    def pair_to_rows(buffer, pair):
        for at in range(4):
            turned = dot(tab[P2], buffer[256 * at : 256 * at + 256, :]).astype(BF16)
            for row in range(16):
                seq, chan, half, high = row // 8, row // 4 % 2, row // 2 % 2, row % 2
                start = pair * 256 + seq * 512 + chan * 128 + half * 64 + at * 16
                rows[pl.ds(pl.multiple_of(start, 16), 16), 128 * high : 128 * high + 128] = turned[
                    row * 16 : row * 16 + 16
                ]

    def spectra(ats):
        blocks = jnp.concatenate(
            [rows[pl.ds(pl.multiple_of(at * 128, 128), 128), :] for at in ats], 1
        )
        step = dot(tab[A2], jnp.concatenate([blocks, blocks], 0))
        return forward(tab, tw, step, len(ats))

    wait_all(og_recv, recv_sem, 0)
    to_rows(og_recv)

    def input_grad(chan, _):
        ats = (chan, chan + 4)
        taps = flt_spec[chan]
        fr, fi = taps[:, :128], taps[:, 128:]
        specs = spectra(ats)
        corrs = []
        for spec in specs:
            sr, si = spec[:, :128], spec[:, 128:]
            corrs.append(jnp.concatenate([fr * sr + fi * si, fr * si - fi * sr], 1))
        grads = inverse(tab, tw, corrs)
        for at, spec, grad in zip(ats, specs, grads, strict=True):
            grad_spec[at] = spec
            rows[pl.ds(pl.multiple_of(at * 128, 128), 128), :] = grad.astype(BF16)
        return 0

    lax.fori_loop(0, 4, input_grad, 0)

    def from_rows(at, _):
        block = jnp.concatenate(
            [rows[pl.ds(pl.multiple_of(row * 64 + at * 16, 16), 16), :] for row in range(16)], 0
        )
        ig_send[pl.ds(pl.multiple_of(at * 256, 256), 256), :] = dot(tab[P2], block).astype(BF16)
        return 0

    lax.fori_loop(0, 4, from_rows, 0, unroll=True)
    send_all(ig_send, ig_recv, 3)
    keep_own(ig_send, ig_recv)

    def part_copy(slot, peer):
        return pltpu.make_async_remote_copy(
            src_ref=fg_part.at[slot],
            dst_ref=fg_recv.at[slot],
            send_sem=fg_send_sem.at[slot],
            recv_sem=fg_recv_sem.at[slot],
            device_id={"rep": peer},
            device_id_type=MESH,
        )

    def filter_grad(chan):
        ats = (chan, chan + 4)
        total_r = total_i = None
        for at, spec in zip(ats, spectra(ats), strict=True):
            grad = grad_spec[at]
            sr, si, gr, gi = spec[:, :128], spec[:, 128:], grad[:, :128], grad[:, 128:]
            real, imag = sr * gr + si * gi, sr * gi - si * gr
            total_r = real if total_r is None else total_r + real
            total_i = imag if total_i is None else total_i + imag
        (part,) = inverse(tab, tw, [jnp.concatenate([total_r, total_i], 1)])
        return part

    for which, (_, target, pair) in enumerate(pairs):
        wait_all(target, recv_sem, 1 + which)
        pair_to_rows(target, pair)

        def filter_grads(step, _):
            chan = 2 * pair + jnp.where(step == 0, 1 - core, core)
            fg_part[2 * which + step] = filter_grad(chan)

            @pl.when(step == 0)
            def _():
                part_copy(2 * which, near).start()

            return 0

        lax.fori_loop(0, 2, filter_grads, 0)
        if which == 0:
            part_copy(0, near).wait()
            fg_part[1] += fg_recv[0]
            part_copy(1, far).start()
    part_copy(1, far).wait()
    part_copy(2, near).wait()
    total = fg_part[3] + fg_recv[2] + fg_recv[1]
    total = total * (1.0 / 512.0)
    for half in range(2):
        for high in range(2):
            fg_out[pl.ds(2 * half + high, 64, stride=4), :] = total[
                half * 64 : half * 64 + 64, high * 128 : high * 128 + 128
            ]
    row = lax.broadcasted_iota(jnp.int32, (256, 256), 0)
    col = lax.broadcasted_iota(jnp.int32, (256, 256), 1)
    chan = row % 64
    origin = chan // 4 * 16 + row // 128 * 8 + chan % 4 * 2 + row // 64 % 2
    back = jnp.where(origin == col, 1.0, 0.0).astype(BF16)
    wait_all(ig_recv, recv_sem, 3)
    for at in range(4):
        turned = dot(back, ig_recv[256 * at : 256 * at + 256, :]).astype(BF16)
        for seq in range(2):
            for half in range(2):
                start = seq * 128 + half * 64
                ig_out[seq, 64 * at : 64 * at + 64, half * 256 : half * 256 + 256] = turned[
                    start : start + 64
                ]
    wait_all(og_send, send_sem, 0)
    wait_all(gi_send0, send_sem, 1)
    wait_all(gi_send1, send_sem, 2)
    wait_all(ig_send, send_sem, 3)


def write_out(ig, fg, ig_hbm, fg_hbm, sem):
    copies = [
        pltpu.make_async_copy(ig, ig_hbm, sem.at[0]),
        pltpu.make_async_copy(fg, fg_hbm, sem.at[1]),
    ]
    for copy in copies:
        copy.start()
    for copy in copies:
        copy.wait()


def local(gated_input, out_grad, filter_taps):
    move, tables = bf16_tables()
    taps = filter_taps.reshape(4, 256, 128).transpose(1, 0, 2).reshape(1024, 128)
    hbm = pl.BlockSpec(memory_space=pltpu.HBM)
    vmem = pl.BlockSpec(memory_space=pltpu.VMEM)
    chunks = pltpu.VMEM((CTX * ROWS, 256), BF16)
    pair_chunks = pltpu.VMEM((CTX * ROWS, 128), BF16)
    input_part, filter_part = pl.pallas_call(
        kernel,
        out_shape=(
            jax.ShapeDtypeStruct((2, 256, 512), BF16),
            jax.ShapeDtypeStruct((256, 128), F32),
        ),
        in_specs=[hbm] * 7,
        out_specs=(vmem, vmem),
        scratch_shapes=[
            pltpu.VMEM((2, 256, 512), BF16),
            pltpu.VMEM((2, 256, 512), BF16),
            pltpu.VMEM((1024, 128), F32),
            pltpu.VMEM((256, 256), BF16),
            pltpu.VMEM((2, 256, 512), BF16),
            pltpu.VMEM((7, 256, 256), BF16),
            pltpu.VMEM((128, 768), F32),
            chunks, pair_chunks, pair_chunks, chunks, chunks, pair_chunks, pair_chunks, chunks,
            chunks,
            pltpu.VMEM((8, 256, 256), F32),
            pltpu.VMEM((4, 256, 256), F32),
            pltpu.VMEM((4, 128, 256), F32),
            pltpu.VMEM((3, 128, 256), F32),
            pltpu.SemaphoreType.DMA((7,)),
            pltpu.SemaphoreType.DMA((4,)),
            pltpu.SemaphoreType.DMA((4,)),
            pltpu.SemaphoreType.DMA((3,)),
            pltpu.SemaphoreType.DMA((3,)),
        ],
        compiler_params=pltpu.CompilerParams(
            collective_id=0, has_side_effects=True, vmem_limit_bytes=40 * 2**20
        ),
    )(
        *(
            pltpu.with_memory_space_constraint(operand, pltpu.HBM)
            for operand in (
                out_grad, gated_input, taps,
                jnp.asarray(move), jnp.asarray(pair_moves()), jnp.asarray(tables), jnp.asarray(f32_tables()),
            )
        )
    )
    input_grad, filter_grad = pl.pallas_call(
        write_out,
        out_shape=(
            jax.ShapeDtypeStruct((2, 256, 512), BF16),
            jax.ShapeDtypeStruct((256, 128), F32),
        ),
        in_specs=[vmem, vmem],
        out_specs=(pl.BlockSpec(memory_space=pl.ANY),) * 2,
        scratch_shapes=[
            pltpu.SemaphoreType.DMA((2,)),
        ],
        compiler_params=pltpu.CompilerParams(vmem_limit_bytes=16 * 2**20),
    )(input_part, filter_part)
    return input_grad, filter_grad.reshape(1, 32768)


def solution(mesh):
    return jax.shard_map(
        local,
        mesh=mesh,
        in_specs=(P("rep", None, "ctx"), P("rep", None, "ctx"), P("ctx", None)),
        out_specs=(P("rep", None, "ctx"), P(("ctx", "rep"), None)),
        check_vma=False,
    )
```
